128 devices in a mesh: segment: 4 (over x), gy: 32 (over y, z, core).
Axes of the slice: x: 4, y: 4, z: 4, core: 2. Of those that a mesh axis runs over, the one named last changes fastest.
Arguments:
- crops: bfloat16 [2, 32, 4, 128, 128], P(None, None, None, 'gy'), may hold values from -6 to 6
- cotangent: bfloat16 [2, 32, 4, 128, 128], P(None, None, None, 'gy'), may hold values from -0.59765625 to 0.59765625
- weights: bfloat16 [4, 2, 27, 32, 32], P('segment'), may hold values from -0.375 to 0.375
Outputs:
- features: bfloat16 [4, 2, 32, 4, 128, 128], P('segment', None, None, None, 'gy')
- weight_grads: float32 [4, 2, 27, 32, 32], P('segment')
- input_grads: float32 [4, 2, 32, 4, 128, 128], P('segment', None, None, None, 'gy')
The draws below stay inside these ranges and needn't reach their ends.
All inputs are finite; a program needn't handle non-finite values.
Results may differ from the reference program's by a relative error of at most 0.025.
Values may be sent and summed in bfloat16 or wider, within the bound.
No kernel may reach another device: no remote copies, remote signals or barrier semaphores. Data moves between devices by JAX's collectives and lax.ppermute only.
A program may use at most 128 MiB of HBM per device.

```python
import jax
import jax.numpy as jnp
from jax import lax

C = 32
MICRO = 2
Z = 4
X = 128
Y = 128


def steps_of(rng, dims, split, smallest, high):
    def one(dim, shards_of):
        steps = jax.random.uniform(jax.random.fold_in(jax.random.fold_in(rng, 6), dim), (shards_of,), jnp.float32, smallest / len(split), high / len(split))
        return jnp.repeat(jnp.exp(steps), dims[dim] // shards_of).reshape((-1,) + (1,) * (len(dims) - dim - 1))

    factor_of = one(*split[0])
    for cut in split[1:]:
        factor_of = factor_of * one(*cut)
    return factor_of


def gaussian(rng, shape, scale, most, split=(), held_as=jnp.bfloat16):
    gain = steps_of(rng, shape, split, -0.22, 0.18) if split else 1.0
    drawn = jax.random.normal(rng, shape, jnp.float32) * scale * gain
    return jnp.minimum(jnp.maximum(drawn, -most), most).astype(held_as)


def setup_inputs(seed: int = 0) -> dict:
    key_of = jax.random.split(jax.random.key(seed), 4)
    crops = gaussian(key_of[0], (MICRO, C, Z, Y, X), 1.0, 6.0, ((3, 32),))
    cotangent = gaussian(key_of[1], (MICRO, C, Z, Y, X), 0.1, 0.59765625, ((3, 32),))
    weights = gaussian(key_of[2], (4, 2, 27, C, C), (9 * C) ** -0.5, 0.375, ((0, 4),))
    return {"crops": crops, "cotangent": cotangent, "weights": weights}


def surround(volume):
    return jnp.pad(volume, ((0, 0), (1, 1), (1, 1), (1, 1)))


def slices_of(padded, plane_shift, row_count):
    planes = padded.shape[1] - 2
    across = padded.shape[3] - 2
    return jnp.stack([padded[:, plane_shift:plane_shift + planes, row_shift:row_shift + row_count, side_shift:side_shift + across] for row_shift in range(3) for side_shift in range(3)])


def convolve(padded, kernel, row_count):
    result = None
    for plane_shift in range(3):
        stacked = slices_of(padded, plane_shift, row_count).astype(jnp.float32)
        tap_weights = kernel[9 * plane_shift:9 * plane_shift + 9].astype(jnp.float32)
        contribution = jnp.einsum("tczyx,tco->ozyx", stacked, tap_weights, precision=lax.Precision.HIGHEST)
        result = contribution if result is None else result + contribution
    return result


def kernel_grads(padded, gradient, row_count):
    pieces = []
    for plane_shift in range(3):
        stacked = slices_of(padded, plane_shift, row_count).astype(jnp.float32)
        pieces.append(jnp.einsum("tczyx,ozyx->tco", stacked, gradient.astype(jnp.float32), precision=lax.Precision.HIGHEST))
    return jnp.concatenate(pieces, 0)


def flipped(kernel):
    return jnp.transpose(jnp.flip(kernel, 0), (0, 2, 1))


def slope(preact):
    logistic = jax.nn.sigmoid(preact)
    return logistic * (1.0 + preact * (1.0 - logistic))


def reference(crops, cotangent, weights):
    row_count = crops.shape[3]
    features = []
    input_grads = []
    weight_grads = jnp.zeros(weights.shape, jnp.float32)
    for micro_index in range(MICRO):
        entries = []
        stored = []
        carried = crops[micro_index]
        for section in range(4):
            entering = carried
            entries.append(entering)
            if section >= 2:
                merged = (entering.astype(jnp.float32) + entries[3 - section].astype(jnp.float32)).astype(jnp.bfloat16)
            else:
                merged = entering
            input_pad = surround(merged)
            pre_first = convolve(input_pad, weights[section, 0], row_count)
            hidden_pad = surround(jax.nn.silu(pre_first).astype(jnp.bfloat16))
            pre_second = convolve(hidden_pad, weights[section, 1], row_count)
            carried = jax.nn.silu(pre_second).astype(jnp.bfloat16)
            stored.append((input_pad, pre_first, hidden_pad, pre_second, carried))
        incoming = cotangent[micro_index]
        deltas = [None, None, None, None]
        sums = [None, None, None, None]
        for section in (3, 2, 1, 0):
            input_pad, pre_first, hidden_pad, pre_second, unused_out = stored[section]
            second_delta = (incoming.astype(jnp.float32) * slope(pre_second)).astype(jnp.bfloat16)
            grad_second = kernel_grads(hidden_pad, second_delta, row_count)
            hidden_delta = convolve(surround(second_delta), flipped(weights[section, 1]), row_count)
            first_delta = (hidden_delta * slope(pre_first)).astype(jnp.bfloat16)
            grad_first = kernel_grads(input_pad, first_delta, row_count)
            weight_grads = weight_grads.at[section].add(jnp.stack([grad_first, grad_second]))
            deltas[section] = convolve(surround(first_delta), flipped(weights[section, 0]), row_count).astype(jnp.bfloat16)
            if section == 1:
                sums[1] = deltas[1].astype(jnp.float32) + deltas[2].astype(jnp.float32)
                incoming = sums[1].astype(jnp.bfloat16)
            elif section == 0:
                sums[0] = deltas[0].astype(jnp.float32) + deltas[3].astype(jnp.float32)
            else:
                sums[section] = deltas[section].astype(jnp.float32)
                incoming = deltas[section]
        input_grads.append(jnp.stack(sums))
        features.append(jnp.stack([stored[section][4] for section in range(4)]))
    return jnp.stack(features, 1), weight_grads, jnp.stack(input_grads, 1)
```

```python
import functools

import jax
import jax.numpy as jnp
from jax import lax
from jax.experimental import pallas as pl
from jax.experimental.pallas import tpu as pltpu
from jax.sharding import PartitionSpec as P

ROWS = 4
WIDTH = 80
CHUNK = 4
SPAN = CHUNK * WIDTH
TOTAL = 36
LANES = 128
F32 = jnp.float32
BF16 = jnp.bfloat16


def sigmoid(v):
    return 0.5 * jnp.tanh(0.5 * v) + 0.5


def slope(v):
    s = sigmoid(v)
    return s * (1.0 + v * (1.0 - s))


def at_row(row):
    return pl.multiple_of(row * WIDTH, 16)


def main_kernel(
    own, oth, near, far, near_other, far_other, pack0, pack1, pack2, pack3,
    out0, out1, out2, out3,
    wpack, crop, cot, feats, merged, hidden, delta, sd, fd, pre1, pre2, w1, wb,
    lx, lxt, block, grads, terms, out_all,
):
    seg = lax.axis_index("segment")
    gy = lax.axis_index("gy")
    core = lax.rem(gy, 2)
    half = lax.div(seg, 2)
    column = lax.rem(lax.broadcasted_iota(jnp.int32, (SPAN, LANES), 0), WIDTH)
    first_column = column == 0
    last_column = column == WIDTH - 1
    strip = ROWS * WIDTH

    for k, pack in enumerate((pack0, pack1, pack2, pack3)):
        wpack[lax.rem(seg - k + 4, 4)] = pack[...]

    def put(dst, row, src, src_row, rows):
        dst[row * WIDTH : (row + rows) * WIDTH, :] = src[src_row * WIDTH : (src_row + rows) * WIDTH, :]

    @pl.when(core == 0)
    def _():
        put(crop, 0, far, 0, 8)
        put(crop, 8, near.at[0], 0, 8)
        put(crop, 16, own.at[0], 0, 4)
        put(crop, 20, oth.at[0], 0, 4)
        put(crop, 24, near_other.at[0], 4, 4)
        put(crop, 28, near_other.at[0], 0, 4)
        put(crop, 32, far_other, 4, 4)
        put(cot, 0, near.at[1], 0, 8)
        put(cot, 8, own.at[1], 0, 4)
        put(cot, 12, oth.at[1], 0, 4)
        put(cot, 16, near_other.at[1], 4, 4)

    @pl.when(core == 1)
    def _():
        put(crop, 0, far_other, 4, 4)
        put(crop, 4, near_other.at[0], 0, 8)
        put(crop, 12, oth.at[0], 0, 4)
        put(crop, 16, own.at[0], 0, 4)
        put(crop, 20, near.at[0], 4, 4)
        put(crop, 24, near.at[0], 0, 4)
        put(crop, 28, far, 4, 4)
        put(crop, 32, far, 0, 4)
        put(cot, 0, near_other.at[1], 4, 4)
        put(cot, 4, oth.at[1], 0, 4)
        put(cot, 8, own.at[1], 0, 4)
        put(cot, 12, near.at[1], 4, 4)
        put(cot, 16, near.at[1], 0, 4)

    er = lax.broadcasted_iota(jnp.int32, (LANES, 4 * LANES), 0)
    ec = lax.broadcasted_iota(jnp.int32, (LANES, 4 * LANES), 1)
    expand = jnp.where(er == lax.shift_right_logical(ec, 2), 1.0, 0.0).astype(BF16)
    cr = lax.broadcasted_iota(jnp.int32, (4 * LANES, LANES), 0)
    cc = lax.broadcasted_iota(jnp.int32, (4 * LANES, LANES), 1)
    collapse = jnp.where(cc == lax.shift_right_logical(cr, 2), 1.0, 0.0).astype(BF16)
    plane = lax.bitwise_and(lax.broadcasted_iota(jnp.int32, (32, LANES), 1), 3)
    on_plane = [plane == z for z in range(4)]

    def build(index, carry):
        w = wpack[lax.div(index, 2), lax.rem(index, 2)]
        lx[...] = jnp.dot(w, expand, preferred_element_type=F32)
        for q in range(7):
            lxt[q * LANES : (q + 1) * LANES, :] = lax.dot_general(
                w[q * 32 : (q + 1) * 32], expand[:32, :LANES], (((0,), (0,)), ((), ())), preferred_element_type=F32
            )
        for dy in range(3):
            for dx in range(3):
                taps = [9 * dz + 3 * dy + dx for dz in range(3)]
                fwd = [lx[t // 4 * 32 : t // 4 * 32 + 32, t % 4 * LANES : (t % 4 + 1) * LANES] for t in taps]
                bwd = [lxt[t * 32 : t * 32 + 32, :] for t in taps]
                for z in range(4):
                    vf = jnp.zeros((32, LANES), F32)
                    vb = jnp.zeros((32, LANES), F32)
                    for dz in range(3):
                        if 0 <= z + 1 - dz < 4:
                            vf = jnp.where(on_plane[z + 1 - dz], fwd[dz], vf)
                        if 0 <= z + dz - 1 < 4:
                            vb = jnp.where(on_plane[z + dz - 1], bwd[dz], vb)
                    block[0, pl.ds(z, 32, stride=4), :] = vf
                    block[1, pl.ds(z, 32, stride=4), :] = vb
                w1[index, dy * LANES : (dy + 1) * LANES, dx * LANES : (dx + 1) * LANES] = block[0].astype(BF16)
                wb[index, (2 - dy) * LANES : (3 - dy) * LANES, (2 - dx) * LANES : (3 - dx) * LANES] = block[1].astype(
                    BF16
                )
        return carry

    lax.fori_loop(0, 8, build, 0)

    def chunks(low, high, body):
        count = -(-(high - low) // CHUNK)

        def step(i, carry):
            body(at_row(jnp.minimum(low + CHUNK * i, high - CHUNK)))
            return carry

        lax.fori_loop(0, count, step, 0)

    def from_left(v):
        return jnp.where(first_column, 0.0, pltpu.roll(v, 1, 0))

    def from_right(v):
        return jnp.where(last_column, 0.0, pltpu.roll(v, SPAN - 1, 0))

    def stacked(src, base):
        return jnp.concatenate(
            [
                src[pl.ds(pl.multiple_of(base - WIDTH, 16), SPAN), :],
                src[pl.ds(base, SPAN), :],
                src[pl.ds(pl.multiple_of(base + WIDTH, 16), SPAN), :],
            ],
            axis=1,
        )

    def conv(src, matrix, low, high, then):
        def body(base):
            p = jnp.dot(stacked(src, base), matrix[...], preferred_element_type=F32)
            then(base, p[:, LANES : 2 * LANES] + from_left(p[:, :LANES]) + from_right(p[:, 2 * LANES :]))

        chunks(low, high, body)

    def clear_outside(dst, low, high):
        top = 16 - ROWS * gy
        bottom = 16 + ROWS * (lax.axis_size("gy") - gy)

        def clear(i, carry):
            dst[pl.ds(at_row(i), WIDTH), :] = jnp.zeros((WIDTH, LANES), BF16)
            return carry

        @pl.when(top > low)
        def _():
            lax.fori_loop(low, jnp.minimum(top, high), clear, 0)

        @pl.when(bottom < high)
        def _():
            lax.fori_loop(jnp.maximum(bottom, low), high, clear, 0)

    for s in range(4):
        source = crop if s == 0 else feats.at[0] if s == 1 else merged.at[s - 2]

        def first(base, v, s=s):
            pre1[s, pl.ds(base, SPAN), :] = v
            hidden[s, pl.ds(base, SPAN), :] = (v * sigmoid(v)).astype(BF16)

        conv(source, w1.at[2 * s], 2 * s + 1, 35 - 2 * s, first)
        clear_outside(hidden.at[s], 2 * s + 1, 35 - 2 * s)

        def second(base, v, s=s):
            pre2[s, pl.ds(base, SPAN), :] = v
            out = (v * sigmoid(v)).astype(BF16)
            feats[s, pl.ds(base, SPAN), :] = out
            if s == 1 or s == 2:
                skip = feats[0, pl.ds(base, SPAN), :] if s == 1 else crop[pl.ds(base, SPAN), :]
                merged[s - 1, pl.ds(base, SPAN), :] = (out.astype(F32) + skip.astype(F32)).astype(BF16)

        conv(hidden.at[s], w1.at[2 * s + 1], 2 * s + 2, 34 - 2 * s, second)
        if s == 0:
            clear_outside(feats.at[0], 2, 34)
        if s == 1 or s == 2:
            clear_outside(merged.at[s - 1], 2 * s + 2, 34 - 2 * s)

    def first_sd(base):
        incoming = cot[pl.ds(pl.multiple_of(base - 8 * WIDTH, 16), SPAN), :]
        sd[pl.ds(base, SPAN), :] = (incoming.astype(F32) * slope(pre2[3, pl.ds(base, SPAN), :])).astype(BF16)

    chunks(8, 28, first_sd)

    own_low = half * 16
    mine = (column >= own_low) & (column < own_low + 64)
    base0 = 16 * WIDTH
    slot_of = lambda s: lax.rem(s - seg + 4, 4)

    def kernel_grads(src, grad, s, which):
        d = jnp.where(mine, grad[base0 : base0 + SPAN, :].astype(F32), 0.0)
        shifted = jnp.concatenate([from_right(d).astype(BF16), d.astype(BF16), from_left(d).astype(BF16)], axis=1)
        product = lax.dot_general(
            stacked(src, base0), shifted, (((0,), (0,)), ((), ())), preferred_element_type=F32
        )
        for dx in range(3):
            grads[dx] = product[:, dx * LANES : (dx + 1) * LANES]
        terms[6 * 32 :, 3 * LANES :] = jnp.zeros((32, LANES), BF16)
        for dy in range(3):
            for dx in range(3):
                rows = [grads[dx, pl.ds(dy * LANES + z, 32, stride=4), :] for z in range(4)]
                for dz in range(3):
                    total = jnp.zeros((32, LANES), F32)
                    for z in range(4):
                        if 0 <= z + 1 - dz < 4:
                            total = jnp.where(on_plane[z + 1 - dz], rows[z], total)
                    t = 9 * dz + 3 * dy + dx
                    terms[t // 4 * 32 : t // 4 * 32 + 32, t % 4 * LANES : (t % 4 + 1) * LANES] = total.astype(BF16)
        packed = jnp.dot(terms[...], collapse, preferred_element_type=F32).astype(BF16)
        out_all[slot_of(s), 512 + 224 * which : 736 + 224 * which, :] = packed

    for s in (3, 2, 1, 0):
        source = crop if s == 0 else feats.at[0] if s == 1 else merged.at[s - 2]
        low, high = 8 + 2 * (3 - s), 28 - 2 * (3 - s)

        def to_first(base, v, s=s):
            fd[pl.ds(base, SPAN), :] = (v * slope(pre1[s, pl.ds(base, SPAN), :])).astype(BF16)

        kernel_grads(hidden.at[s], sd, s, 1)
        conv(sd, wb.at[2 * s + 1], low + 1, high - 1, to_first)
        clear_outside(fd, low + 1, high - 1)
        kernel_grads(source, fd, s, 0)

        def to_delta(base, v, s=s):
            out = v.astype(BF16)
            if s == 1 or s == 0:
                other = delta[2 if s == 1 else 3, pl.ds(base, SPAN), :]
                out = (out.astype(F32) + other.astype(F32)).astype(BF16)
            delta[s, pl.ds(base, SPAN), :] = out
            if s > 0:
                sd[pl.ds(base, SPAN), :] = (
                    out.astype(F32) * slope(pre2[s - 1, pl.ds(base, SPAN), :])
                ).astype(BF16)

        conv(fd, wb.at[2 * s], low + 2, high - 2, to_delta)
        if s > 0:
            clear_outside(sd, low + 2, high - 2)

    for s in range(4):
        for y in range(ROWS):
            place = pl.ds(pl.multiple_of(base0 + y * WIDTH + own_low, 16), 64)
            out_all[slot_of(s), 64 * y : 64 * y + 64, :] = feats[s, place, :]
            out_all[slot_of(s), 256 + 64 * y : 320 + 64 * y, :] = delta[s, place, :]
    for k, out in enumerate((out0, out1, out2, out3)):
        out[...] = out_all[k]


def main_call(*operands):
    acts = (TOTAL * WIDTH, LANES)
    vmem = pl.BlockSpec(memory_space=pltpu.VMEM)
    return pl.pallas_call(
        main_kernel,
        out_shape=[jax.ShapeDtypeStruct((960, LANES), BF16)] * 4,
        in_specs=[vmem] * 10,
        out_specs=[vmem] * 4,
        scratch_shapes=[
            pltpu.VMEM((4, 2, 224, LANES), BF16),
            pltpu.VMEM(acts, BF16),
            pltpu.VMEM((20 * WIDTH, LANES), BF16),
            pltpu.VMEM((4,) + acts, BF16),
            pltpu.VMEM((2,) + acts, BF16),
            pltpu.VMEM((4,) + acts, BF16),
            pltpu.VMEM((4,) + acts, BF16),
            pltpu.VMEM(acts, BF16),
            pltpu.VMEM(acts, BF16),
            pltpu.VMEM((4,) + acts, F32),
            pltpu.VMEM((4,) + acts, F32),
            pltpu.VMEM((8, 3 * LANES, 3 * LANES), BF16),
            pltpu.VMEM((8, 3 * LANES, 3 * LANES), BF16),
            pltpu.VMEM((224, 4 * LANES), F32),
            pltpu.VMEM((7 * LANES, LANES), F32),
            pltpu.VMEM((2, LANES, LANES), F32),
            pltpu.VMEM((3, 3 * LANES, LANES), F32),
            pltpu.VMEM((224, 4 * LANES), BF16),
            pltpu.VMEM((4, 960, LANES), BF16),
        ],
        compiler_params=pltpu.CompilerParams(vmem_limit_bytes=56 * 1024 * 1024),
        name="sections",
    )(*operands)


def rotated(value, axis, group, step, stride):
    count = lax.axis_size(axis)

    def target(i):
        place = i // stride % group
        return i + ((place + step) % group - place) * stride

    return lax.ppermute(value, axis, [(i, target(i)) for i in range(count)])


def local(crops, cotangent, weights):
    micro_count, channels, planes, rows, across = crops.shape
    seg = lax.axis_index("segment")
    micro, half = seg % 2, seg // 2
    devices = lax.axis_size("gy")
    swap = [(i, i ^ 1) for i in range(devices)]

    def tile(volume):
        field = lax.dynamic_index_in_dim(volume, micro, 0, keepdims=False)
        field = jnp.transpose(field, (2, 3, 0, 1)).reshape(rows, across, channels * planes)
        return lax.dynamic_slice_in_dim(field, half * 48, WIDTH, 1).reshape(rows * WIDTH, channels * planes)

    own = jnp.stack([tile(crops), tile(cotangent)])
    packed = jnp.pad(weights[0], ((0, 0), (0, 1), (0, 0), (0, 0))).reshape(2, 7, 4, channels, channels)
    packed = jnp.transpose(packed, (0, 1, 3, 2, 4)).reshape(2, 7 * channels, 4 * channels)

    oth = lax.ppermute(own, "gy", swap)
    block = jnp.concatenate([own, oth], axis=1)

    def outward(distance):
        return [
            (i, i + 2 * distance * (1 if i % 2 == 0 else -1))
            for i in range(devices)
            if 0 <= i + 2 * distance * (1 if i % 2 == 0 else -1) < devices
        ]

    near = lax.ppermute(block, "gy", outward(1))
    far = lax.ppermute(block[0], "gy", outward(2))
    others = [rotated(packed, "segment", 4, k, 1) for k in (1, 2, 3)]
    near_other = lax.ppermute(near, "gy", swap)
    far_other = lax.ppermute(far, "gy", swap)
    outs = main_call(own, oth, near, far, near_other, far_other, packed, *others)
    arrived = [outs[0]] + [rotated(outs[k], "segment", 4, k, 1) for k in (1, 2, 3)]
    by_step = jnp.stack(arrived)
    total = by_step[:, 512:].astype(F32).sum(0)
    total = total + lax.ppermute(total.astype(BF16), "gy", swap).astype(F32)
    for stride in (2, 8):
        mine = total.astype(BF16)
        total = mine.astype(F32)
        for k in (1, 2, 3):
            total = total + rotated(mine, "gy", 4, k, stride).astype(F32)
    grads = total.reshape(2, 7, channels, 4, channels).transpose(0, 1, 3, 2, 4)
    grads = grads.reshape(2, 28, channels, channels)[:, :27]

    fields = by_step[:, :512]
    by_source = jnp.stack([lax.dynamic_index_in_dim(fields, (seg - j) % 4, 0, keepdims=False) for j in range(4)])
    fields = by_source.reshape(2, 2, 2, rows, across // 2, channels, planes)
    fields = jnp.transpose(fields, (2, 1, 5, 6, 3, 0, 4)).reshape(2, micro_count, channels, planes, rows, across)
    return fields[0][None], grads[None], fields[1].astype(F32)[None]


def solution(mesh):
    return jax.shard_map(
        local,
        mesh=mesh,
        in_specs=(
            P(None, None, None, "gy", None),
            P(None, None, None, "gy", None),
            P("segment", None, None, None, None),
        ),
        out_specs=(
            P("segment", None, None, None, "gy", None),
            P("segment", None, None, None, None),
            P("segment", None, None, None, "gy", None),
        ),
        check_vma=False,
    )
```

```python
import jax
import jax.numpy as jnp
from jax import lax
from jax.experimental import pallas as pl
from jax.experimental.pallas import tpu as pltpu
from jax.sharding import PartitionSpec as P

ROWS = 4
WIDTH = 80
SINGLE = 12
TOTAL = 36
LANES = 128
F32 = jnp.float32
BF16 = jnp.bfloat16


def sigmoid(v):
    return 0.5 * jnp.tanh(0.5 * v) + 0.5


def slope(v):
    s = sigmoid(v)
    return s * (1.0 + v * (1.0 - s))


def at_row(row):
    return pl.multiple_of(row * WIDTH, 16)


def constants():
    er = lax.broadcasted_iota(jnp.int32, (LANES, 4 * LANES), 0)
    ec = lax.broadcasted_iota(jnp.int32, (LANES, 4 * LANES), 1)
    expand = jnp.where(er == lax.shift_right_logical(ec, 2), 1.0, 0.0).astype(BF16)
    cr = lax.broadcasted_iota(jnp.int32, (4 * LANES, LANES), 0)
    cc = lax.broadcasted_iota(jnp.int32, (4 * LANES, LANES), 1)
    collapse = jnp.where(cc == lax.shift_right_logical(cr, 2), 1.0, 0.0).astype(BF16)
    plane = lax.bitwise_and(lax.broadcasted_iota(jnp.int32, (32, LANES), 1), 3)
    return expand, collapse, [plane == z for z in range(4)]


def build_kernel(pack0, pack1, pack2, pack3, w1, wb, wpack, lx, lxt, block):
    seg = lax.axis_index("segment")
    for k, pack in enumerate((pack0, pack1, pack2, pack3)):
        wpack[lax.rem(seg - k + 4, 4)] = pack[...]
    expand, _, on_plane = constants()

    def build(index, carry):
        w = wpack[lax.div(index, 2), lax.rem(index, 2)]
        lx[...] = jnp.dot(w, expand, preferred_element_type=F32)
        for q in range(7):
            lxt[q * LANES : (q + 1) * LANES, :] = lax.dot_general(
                w[q * 32 : (q + 1) * 32], expand[:32, :LANES], (((0,), (0,)), ((), ())), preferred_element_type=F32
            )
        for dy in range(3):
            for dx in range(3):
                taps = [9 * dz + 3 * dy + dx for dz in range(3)]
                fwd = [lx[t // 4 * 32 : t // 4 * 32 + 32, t % 4 * LANES : (t % 4 + 1) * LANES] for t in taps]
                bwd = [lxt[t * 32 : t * 32 + 32, :] for t in taps]
                for z in range(4):
                    vf = jnp.zeros((32, LANES), F32)
                    vb = jnp.zeros((32, LANES), F32)
                    for dz in range(3):
                        if 0 <= z + 1 - dz < 4:
                            vf = jnp.where(on_plane[z + 1 - dz], fwd[dz], vf)
                        if 0 <= z + dz - 1 < 4:
                            vb = jnp.where(on_plane[z + dz - 1], bwd[dz], vb)
                    block[0, pl.ds(z, 32, stride=4), :] = vf
                    block[1, pl.ds(z, 32, stride=4), :] = vb
                w1[index, dy * LANES : (dy + 1) * LANES, dx * LANES : (dx + 1) * LANES] = block[0].astype(BF16)
                wb[index, (2 - dy) * LANES : (3 - dy) * LANES, (2 - dx) * LANES : (3 - dx) * LANES] = block[1].astype(
                    BF16
                )
        return carry

    lax.fori_loop(0, 8, build, 0)


def main_kernel(
    own, oth, near, far, near_other, far_other, w1, wb,
    out0, out1, out2, out3, keep0, keep1, keep2, keep3, send,
    crop, cot, feats, merged, hidden, delta, sd, fd, pre1, pre2, grads, terms, out_all, wg_all,
):
    seg = lax.axis_index("segment")
    gy = lax.axis_index("gy")
    core = lax.rem(gy, 2)
    half = lax.div(seg, 2)
    column = lax.broadcasted_iota(jnp.int32, (1, WIDTH, LANES), 1)

    def put(dst, row, src, src_row, rows):
        dst[row * WIDTH : (row + rows) * WIDTH, :] = src[src_row * WIDTH : (src_row + rows) * WIDTH, :]

    @pl.when(core == 0)
    def _():
        put(crop, 0, far, 0, 8)
        put(crop, 8, near.at[0], 0, 8)
        put(crop, 16, own.at[0], 0, 4)
        put(crop, 20, oth.at[0], 0, 4)
        put(crop, 24, near_other.at[0], 4, 4)
        put(crop, 28, near_other.at[0], 0, 4)
        put(crop, 32, far_other, 4, 4)
        put(cot, 0, near.at[1], 0, 8)
        put(cot, 8, own.at[1], 0, 4)
        put(cot, 12, oth.at[1], 0, 4)
        put(cot, 16, near_other.at[1], 4, 4)

    @pl.when(core == 1)
    def _():
        put(crop, 0, far_other, 4, 4)
        put(crop, 4, near_other.at[0], 0, 8)
        put(crop, 12, oth.at[0], 0, 4)
        put(crop, 16, own.at[0], 0, 4)
        put(crop, 20, near.at[0], 4, 4)
        put(crop, 24, near.at[0], 0, 4)
        put(crop, 28, far, 4, 4)
        put(crop, 32, far, 0, 4)
        put(cot, 0, near_other.at[1], 4, 4)
        put(cot, 4, oth.at[1], 0, 4)
        put(cot, 8, own.at[1], 0, 4)
        put(cot, 12, near.at[1], 4, 4)
        put(cot, 16, near.at[1], 0, 4)

    _, collapse, on_plane = constants()

    def chunks(low, high, body):
        count = 1 if high - low <= SINGLE else 2
        rows = (high - low) // count

        def step(i, carry):
            body(at_row(low + rows * i), rows * WIDTH)
            return carry

        lax.fori_loop(0, count, step, 0)

    def by_rows(v):
        return v.reshape(v.shape[0] // WIDTH, WIDTH, LANES)

    def from_left(v):
        return jnp.where(column == 0, 0.0, pltpu.roll(by_rows(v), 1, 1)).reshape(v.shape)

    def from_right(v):
        return jnp.where(column == WIDTH - 1, 0.0, pltpu.roll(by_rows(v), WIDTH - 1, 1)).reshape(v.shape)

    def stacked(src, base, span):
        return jnp.concatenate(
            [
                src[pl.ds(pl.multiple_of(base - WIDTH, 16), span), :],
                src[pl.ds(base, span), :],
                src[pl.ds(pl.multiple_of(base + WIDTH, 16), span), :],
            ],
            axis=1,
        )

    def conv(src, matrix, low, high, then):
        def body(base, span):
            p = jnp.dot(stacked(src, base, span), matrix[...], preferred_element_type=F32)
            then(base, span, p[:, LANES : 2 * LANES] + from_left(p[:, :LANES]) + from_right(p[:, 2 * LANES :]))

        chunks(low, high, body)

    def clear_outside(dst, low, high):
        top = 16 - ROWS * gy
        bottom = 16 + ROWS * (lax.axis_size("gy") - gy)

        def clear(i, carry):
            dst[pl.ds(at_row(i), WIDTH), :] = jnp.zeros((WIDTH, LANES), BF16)
            return carry

        @pl.when(top > low)
        def _():
            lax.fori_loop(low, jnp.minimum(top, high), clear, 0)

        @pl.when(bottom < high)
        def _():
            lax.fori_loop(jnp.maximum(bottom, low), high, clear, 0)

    for s in range(4):
        source = crop if s == 0 else feats.at[0] if s == 1 else merged.at[s - 2]

        def first(base, span, v, s=s):
            pre1[s, pl.ds(base, span), :] = v
            hidden[s, pl.ds(base, span), :] = (v * sigmoid(v)).astype(BF16)

        conv(source, w1.at[2 * s], 2 * s + 1, 35 - 2 * s, first)
        clear_outside(hidden.at[s], 2 * s + 1, 35 - 2 * s)

        def second(base, span, v, s=s):
            pre2[s, pl.ds(base, span), :] = v
            out = (v * sigmoid(v)).astype(BF16)
            feats[s, pl.ds(base, span), :] = out
            if s == 1 or s == 2:
                skip = feats[0, pl.ds(base, span), :] if s == 1 else crop[pl.ds(base, span), :]
                merged[s - 1, pl.ds(base, span), :] = (out.astype(F32) + skip.astype(F32)).astype(BF16)

        conv(hidden.at[s], w1.at[2 * s + 1], 2 * s + 2, 34 - 2 * s, second)
        if s == 0:
            clear_outside(feats.at[0], 2, 34)
        if s == 1 or s == 2:
            clear_outside(merged.at[s - 1], 2 * s + 2, 34 - 2 * s)

    def first_sd(base, span):
        incoming = cot[pl.ds(pl.multiple_of(base - 8 * WIDTH, 16), span), :]
        sd[pl.ds(base, span), :] = (incoming.astype(F32) * slope(pre2[3, pl.ds(base, span), :])).astype(BF16)

    chunks(8, 28, first_sd)

    own_low = half * 16
    mine = (column >= own_low) & (column < own_low + 64)
    base0 = 16 * WIDTH
    span = ROWS * WIDTH
    slot_of = lambda s: lax.rem(s - seg + 4, 4)

    def kernel_grads(src, grad, s, which):
        d = jnp.where(mine, by_rows(grad[base0 : base0 + span, :].astype(F32)), 0.0).reshape(span, LANES)
        shifted = jnp.concatenate([from_right(d).astype(BF16), d.astype(BF16), from_left(d).astype(BF16)], axis=1)
        product = lax.dot_general(
            stacked(src, base0, span), shifted, (((0,), (0,)), ((), ())), preferred_element_type=F32
        )
        for dx in range(3):
            grads[dx] = product[:, dx * LANES : (dx + 1) * LANES]
        terms[6 * 32 :, 3 * LANES :] = jnp.zeros((32, LANES), BF16)
        for dy in range(3):
            for dx in range(3):
                rows = [grads[dx, pl.ds(dy * LANES + z, 32, stride=4), :] for z in range(4)]
                for dz in range(3):
                    total = jnp.zeros((32, LANES), F32)
                    for z in range(4):
                        if 0 <= z + 1 - dz < 4:
                            total = jnp.where(on_plane[z + 1 - dz], rows[z], total)
                    t = 9 * dz + 3 * dy + dx
                    terms[t // 4 * 32 : t // 4 * 32 + 32, t % 4 * LANES : (t % 4 + 1) * LANES] = total.astype(BF16)
        packed = jnp.dot(terms[...], collapse, preferred_element_type=F32).astype(BF16)
        wg_all[which, slot_of(s)] = packed

    for s in (3, 2, 1, 0):
        source = crop if s == 0 else feats.at[0] if s == 1 else merged.at[s - 2]
        low, high = 8 + 2 * (3 - s), 28 - 2 * (3 - s)

        def to_first(base, span, v, s=s):
            fd[pl.ds(base, span), :] = (v * slope(pre1[s, pl.ds(base, span), :])).astype(BF16)

        kernel_grads(hidden.at[s], sd, s, 1)
        conv(sd, wb.at[2 * s + 1], low + 1, high - 1, to_first)
        clear_outside(fd, low + 1, high - 1)
        kernel_grads(source, fd, s, 0)

        def to_delta(base, span, v, s=s):
            out = v.astype(BF16)
            if s == 1 or s == 0:
                other = delta[2 if s == 1 else 3, pl.ds(base, span), :]
                out = (out.astype(F32) + other.astype(F32)).astype(BF16)
            delta[s, pl.ds(base, span), :] = out
            if s > 0:
                sd[pl.ds(base, span), :] = (
                    out.astype(F32) * slope(pre2[s - 1, pl.ds(base, span), :])
                ).astype(BF16)

        conv(fd, wb.at[2 * s], low + 2, high - 2, to_delta)
        if s > 0:
            clear_outside(sd, low + 2, high - 2)

    for s in range(4):
        for y in range(ROWS):
            place = pl.ds(pl.multiple_of(base0 + y * WIDTH + own_low, 16), 64)
            out_all[slot_of(s), 64 * y : 64 * y + 64, :] = feats[s, place, :]
            out_all[slot_of(s), 256 + 64 * y : 320 + 64 * y, :] = delta[s, place, :]
    for k, out in enumerate((out0, out1, out2, out3)):
        out[...] = out_all[k]
    for k, keep in enumerate((keep0, keep1, keep2, keep3)):
        keep[...] = wg_all[core, k]
    send[...] = wg_all[1 - core]


VMEM = pl.BlockSpec(memory_space=pltpu.VMEM)
MATRICES = (8, 3 * LANES, 3 * LANES)


def build_call(*packs):
    return pl.pallas_call(
        build_kernel,
        out_shape=[jax.ShapeDtypeStruct(MATRICES, BF16)] * 2,
        in_specs=[VMEM] * 4,
        out_specs=[VMEM] * 2,
        scratch_shapes=[
            pltpu.VMEM((4, 2, 224, LANES), BF16),
            pltpu.VMEM((224, 4 * LANES), F32),
            pltpu.VMEM((7 * LANES, LANES), F32),
            pltpu.VMEM((2, LANES, LANES), F32),
        ],
        compiler_params=pltpu.CompilerParams(vmem_limit_bytes=8 * 1024 * 1024),
        cost_estimate=pl.CostEstimate(flops=5_000_000_000, bytes_accessed=10_000_000, transcendentals=0),
        name="banded",
    )(*packs)


def main_call(*operands):
    acts = (TOTAL * WIDTH, LANES)
    return pl.pallas_call(
        main_kernel,
        out_shape=[jax.ShapeDtypeStruct((512, LANES), BF16)] * 4
        + [jax.ShapeDtypeStruct((224, LANES), BF16)] * 4
        + [jax.ShapeDtypeStruct((4, 224, LANES), BF16)],
        in_specs=[VMEM] * 8,
        out_specs=[VMEM] * 9,
        scratch_shapes=[
            pltpu.VMEM(acts, BF16),
            pltpu.VMEM((20 * WIDTH, LANES), BF16),
            pltpu.VMEM((4,) + acts, BF16),
            pltpu.VMEM((2,) + acts, BF16),
            pltpu.VMEM((4,) + acts, BF16),
            pltpu.VMEM((4,) + acts, BF16),
            pltpu.VMEM(acts, BF16),
            pltpu.VMEM(acts, BF16),
            pltpu.VMEM((4,) + acts, F32),
            pltpu.VMEM((4,) + acts, F32),
            pltpu.VMEM((3, 3 * LANES, LANES), F32),
            pltpu.VMEM((224, 4 * LANES), BF16),
            pltpu.VMEM((4, 512, LANES), BF16),
            pltpu.VMEM((2, 4, 224, LANES), BF16),
        ],
        compiler_params=pltpu.CompilerParams(vmem_limit_bytes=40 * 1024 * 1024),
        cost_estimate=pl.CostEstimate(flops=20_000_000_000, bytes_accessed=10_000_000, transcendentals=0),
        name="sections",
    )(*operands)


def rotated(value, axis, group, step, stride):
    count = lax.axis_size(axis)

    def target(i):
        place = i // stride % group
        return i + ((place + step) % group - place) * stride

    return lax.ppermute(value, axis, [(i, target(i)) for i in range(count)])


def local(crops, cotangent, weights):
    micro_count, channels, planes, rows, across = crops.shape
    seg = lax.axis_index("segment")
    micro, half = seg % 2, seg // 2
    devices = lax.axis_size("gy")
    swap = [(i, i ^ 1) for i in range(devices)]

    def tile(volume):
        field = lax.dynamic_index_in_dim(volume, micro, 0, keepdims=False)
        field = jnp.transpose(field, (2, 3, 0, 1)).reshape(rows, across, channels * planes)
        return lax.dynamic_slice_in_dim(field, half * 48, WIDTH, 1).reshape(rows * WIDTH, channels * planes)

    own = jnp.stack([tile(crops), tile(cotangent)])
    packed = jnp.pad(weights[0], ((0, 0), (0, 1), (0, 0), (0, 0))).reshape(2, 7, 4, channels, channels)
    packed = jnp.transpose(packed, (0, 1, 3, 2, 4)).reshape(2, 7 * channels, 4 * channels)

    oth = lax.ppermute(own, "gy", swap)
    block = jnp.concatenate([own, oth], axis=1)

    def outward(distance):
        return [
            (i, i + 2 * distance * (1 if i % 2 == 0 else -1))
            for i in range(devices)
            if 0 <= i + 2 * distance * (1 if i % 2 == 0 else -1) < devices
        ]

    near = lax.ppermute(block, "gy", outward(1))
    far = lax.ppermute(block[0], "gy", outward(2))
    others = [rotated(packed, "segment", 4, k, 1) for k in (1, 2, 3)]
    near_other = lax.ppermute(near, "gy", swap)
    far_other = lax.ppermute(far, "gy", swap)
    w1, wb = build_call(packed, *others)
    outs = main_call(own, oth, near, far, near_other, far_other, w1, wb)
    fields, keep, send = outs[:4], outs[4:8], outs[8]

    got = lax.ppermute(send, "gy", swap)
    part = [(keep[k].astype(F32) + got[k].astype(F32)).astype(BF16) for k in range(4)]
    total = part[0].astype(F32)
    for k in (1, 2, 3):
        total = total + rotated(part[k], "segment", 4, k, 1).astype(F32)
    for stride in (2, 8):
        mine = total.astype(BF16)
        total = mine.astype(F32)
        for k in (1, 2, 3):
            total = total + rotated(mine, "gy", 4, k, stride).astype(F32)
    mine = total.astype(BF16)
    other = lax.ppermute(mine, "gy", swap)
    low_core = lax.axis_index("gy") % 2 == 0
    both = jnp.stack([jnp.where(low_core, mine, other), jnp.where(low_core, other, mine)])
    grads = both.reshape(2, 7, channels, 4, channels).transpose(0, 1, 3, 2, 4)
    grads = grads.reshape(2, 28, channels, channels)[:, :27].astype(F32)

    by_step = jnp.stack([fields[0]] + [rotated(fields[k], "segment", 4, k, 1) for k in (1, 2, 3)])
    by_source = jnp.stack([lax.dynamic_index_in_dim(by_step, (seg - j) % 4, 0, keepdims=False) for j in range(4)])
    fields = by_source.reshape(2, 2, 2, rows, across // 2, channels, planes)
    fields = jnp.transpose(fields, (2, 1, 5, 6, 3, 0, 4)).reshape(2, micro_count, channels, planes, rows, across)
    return fields[0][None], grads[None], fields[1].astype(F32)[None]


def solution(mesh):
    return jax.shard_map(
        local,
        mesh=mesh,
        in_specs=(
            P(None, None, None, "gy", None),
            P(None, None, None, "gy", None),
            P("segment", None, None, None, None),
        ),
        out_specs=(
            P("segment", None, None, None, "gy", None),
            P("segment", None, None, None, None),
            P("segment", None, None, None, "gy", None),
        ),
        check_vma=False,
    )
```

```python
import jax
import jax.numpy as jnp
from jax import lax
from jax.experimental import pallas as pl
from jax.experimental.pallas import tpu as pltpu
from jax.sharding import PartitionSpec as P

ROWS = 4
WIDTH = 80
SINGLE = 12
TOTAL = 36
LANES = 128
F32 = jnp.float32
BF16 = jnp.bfloat16


def sigmoid(v):
    return 0.5 * jnp.tanh(0.5 * v) + 0.5


def slope(v):
    s = sigmoid(v)
    return s * (1.0 + v * (1.0 - s))


def at_row(row):
    return pl.multiple_of(row * WIDTH, 16)


def constants():
    er = lax.broadcasted_iota(jnp.int32, (LANES, 4 * LANES), 0)
    ec = lax.broadcasted_iota(jnp.int32, (LANES, 4 * LANES), 1)
    expand = jnp.where(er == lax.shift_right_logical(ec, 2), 1.0, 0.0).astype(BF16)
    cr = lax.broadcasted_iota(jnp.int32, (4 * LANES, LANES), 0)
    cc = lax.broadcasted_iota(jnp.int32, (4 * LANES, LANES), 1)
    collapse = jnp.where(cc == lax.shift_right_logical(cr, 2), 1.0, 0.0).astype(BF16)
    plane = lax.bitwise_and(lax.broadcasted_iota(jnp.int32, (32, LANES), 1), 3)
    return expand, collapse, [plane == z for z in range(4)]


def build_kernel(pack0, pack1, pack2, pack3, w1, wb, wpack, lx, lxt, block):
    seg = lax.axis_index("segment")
    for k, pack in enumerate((pack0, pack1, pack2, pack3)):
        wpack[lax.rem(seg - k + 4, 4)] = pack[...]
    expand, _, on_plane = constants()

    def build(index, carry):
        w = wpack[lax.div(index, 2), lax.rem(index, 2)]
        lx[...] = jnp.dot(w, expand, preferred_element_type=F32)
        for q in range(7):
            lxt[q * LANES : (q + 1) * LANES, :] = lax.dot_general(
                w[q * 32 : (q + 1) * 32], expand[:32, :LANES], (((0,), (0,)), ((), ())), preferred_element_type=F32
            )
        for dy in range(3):
            for dx in range(3):
                taps = [9 * dz + 3 * dy + dx for dz in range(3)]
                fwd = [lx[t // 4 * 32 : t // 4 * 32 + 32, t % 4 * LANES : (t % 4 + 1) * LANES] for t in taps]
                bwd = [lxt[t * 32 : t * 32 + 32, :] for t in taps]
                for z in range(4):
                    vf = jnp.zeros((32, LANES), F32)
                    vb = jnp.zeros((32, LANES), F32)
                    for dz in range(3):
                        if 0 <= z + 1 - dz < 4:
                            vf = jnp.where(on_plane[z + 1 - dz], fwd[dz], vf)
                        if 0 <= z + dz - 1 < 4:
                            vb = jnp.where(on_plane[z + dz - 1], bwd[dz], vb)
                    block[0, pl.ds(z, 32, stride=4), :] = vf
                    block[1, pl.ds(z, 32, stride=4), :] = vb
                w1[index, dy * LANES : (dy + 1) * LANES, dx * LANES : (dx + 1) * LANES] = block[0].astype(BF16)
                wb[index, (2 - dy) * LANES : (3 - dy) * LANES, (2 - dx) * LANES : (3 - dx) * LANES] = block[1].astype(
                    BF16
                )
        return carry

    lax.fori_loop(0, 8, build, 0)


def main_kernel(
    own, oth, near, far, near_other, far_other, w1, wb,
    out0, out1, out2, out3, keep0, keep1, keep2, keep3, send,
    crop, cot, feats, merged, hidden, delta, sd, fd, pre1, pre2, grads, terms, out_all, wg_all,
):
    seg = lax.axis_index("segment")
    gy = lax.axis_index("gy")
    core = lax.rem(gy, 2)
    half = lax.div(seg, 2)
    column = lax.broadcasted_iota(jnp.int32, (1, WIDTH, LANES), 1)

    def put(dst, row, src, src_row, rows):
        dst[row * WIDTH : (row + rows) * WIDTH, :] = src[src_row * WIDTH : (src_row + rows) * WIDTH, :]

    @pl.when(core == 0)
    def _():
        put(crop, 0, far, 0, 8)
        put(crop, 8, near.at[0], 0, 8)
        put(crop, 16, own.at[0], 0, 4)
        put(crop, 20, oth.at[0], 0, 4)
        put(crop, 24, near_other.at[0], 4, 4)
        put(crop, 28, near_other.at[0], 0, 4)
        put(crop, 32, far_other, 4, 4)
        put(cot, 0, near.at[1], 0, 8)
        put(cot, 8, own.at[1], 0, 4)
        put(cot, 12, oth.at[1], 0, 4)
        put(cot, 16, near_other.at[1], 4, 4)

    @pl.when(core == 1)
    def _():
        put(crop, 0, far_other, 4, 4)
        put(crop, 4, near_other.at[0], 0, 8)
        put(crop, 12, oth.at[0], 0, 4)
        put(crop, 16, own.at[0], 0, 4)
        put(crop, 20, near.at[0], 4, 4)
        put(crop, 24, near.at[0], 0, 4)
        put(crop, 28, far, 4, 4)
        put(crop, 32, far, 0, 4)
        put(cot, 0, near_other.at[1], 4, 4)
        put(cot, 4, oth.at[1], 0, 4)
        put(cot, 8, own.at[1], 0, 4)
        put(cot, 12, near.at[1], 4, 4)
        put(cot, 16, near.at[1], 0, 4)

    _, collapse, on_plane = constants()

    def chunks(low, high, body):
        count = 1 if high - low <= SINGLE else 2
        rows = (high - low) // count

        def step(i, carry):
            body(at_row(low + rows * i), rows * WIDTH)
            return carry

        lax.fori_loop(0, count, step, 0)

    def by_rows(v):
        return v.reshape(v.shape[0] // WIDTH, WIDTH, LANES)

    def from_left(v):
        return jnp.where(column == 0, 0.0, pltpu.roll(by_rows(v), 1, 1)).reshape(v.shape)

    def from_right(v):
        return jnp.where(column == WIDTH - 1, 0.0, pltpu.roll(by_rows(v), WIDTH - 1, 1)).reshape(v.shape)

    def stacked(src, base, span):
        return jnp.concatenate(
            [
                src[pl.ds(pl.multiple_of(base - WIDTH, 16), span), :],
                src[pl.ds(base, span), :],
                src[pl.ds(pl.multiple_of(base + WIDTH, 16), span), :],
            ],
            axis=1,
        )

    def conv(src, matrix, low, high, then):
        def body(base, span):
            p = jnp.dot(stacked(src, base, span), matrix[...], preferred_element_type=F32)
            then(base, span, p[:, LANES : 2 * LANES] + from_left(p[:, :LANES]) + from_right(p[:, 2 * LANES :]))

        chunks(low, high, body)

    def clear_outside(dst, low, high):
        top = 16 - ROWS * gy
        bottom = 16 + ROWS * (lax.axis_size("gy") - gy)

        def clear(i, carry):
            dst[pl.ds(at_row(i), WIDTH), :] = jnp.zeros((WIDTH, LANES), BF16)
            return carry

        @pl.when(top > low)
        def _():
            lax.fori_loop(low, jnp.minimum(top, high), clear, 0)

        @pl.when(bottom < high)
        def _():
            lax.fori_loop(jnp.maximum(bottom, low), high, clear, 0)

    for s in range(4):
        source = crop if s == 0 else feats.at[0] if s == 1 else merged.at[s - 2]

        def first(base, span, v, s=s):
            pre1[s, pl.ds(base, span), :] = v
            hidden[s, pl.ds(base, span), :] = (v * sigmoid(v)).astype(BF16)

        conv(source, w1.at[2 * s], 2 * s + 1, 35 - 2 * s, first)
        clear_outside(hidden.at[s], 2 * s + 1, 35 - 2 * s)

        def second(base, span, v, s=s):
            pre2[s, pl.ds(base, span), :] = v
            out = (v * sigmoid(v)).astype(BF16)
            feats[s, pl.ds(base, span), :] = out
            if s == 1 or s == 2:
                skip = feats[0, pl.ds(base, span), :] if s == 1 else crop[pl.ds(base, span), :]
                merged[s - 1, pl.ds(base, span), :] = (out.astype(F32) + skip.astype(F32)).astype(BF16)

        conv(hidden.at[s], w1.at[2 * s + 1], 2 * s + 2, 34 - 2 * s, second)
        if s == 0:
            clear_outside(feats.at[0], 2, 34)
        if s == 1 or s == 2:
            clear_outside(merged.at[s - 1], 2 * s + 2, 34 - 2 * s)

    def first_sd(base, span):
        incoming = cot[pl.ds(pl.multiple_of(base - 8 * WIDTH, 16), span), :]
        sd[pl.ds(base, span), :] = (incoming.astype(F32) * slope(pre2[3, pl.ds(base, span), :])).astype(BF16)

    chunks(8, 28, first_sd)

    own_low = half * 16
    mine = (column >= own_low) & (column < own_low + 64)
    base0 = 16 * WIDTH
    span = ROWS * WIDTH
    slot_of = lambda s: lax.rem(s - seg + 4, 4)

    def kernel_grads(src, grad, s, which):
        d = jnp.where(mine, by_rows(grad[base0 : base0 + span, :].astype(F32)), 0.0).reshape(span, LANES)
        shifted = jnp.concatenate([from_right(d).astype(BF16), d.astype(BF16), from_left(d).astype(BF16)], axis=1)
        product = lax.dot_general(
            stacked(src, base0, span), shifted, (((0,), (0,)), ((), ())), preferred_element_type=F32
        )
        for dx in range(3):
            grads[dx] = product[:, dx * LANES : (dx + 1) * LANES]
        terms[6 * 32 :, 3 * LANES :] = jnp.zeros((32, LANES), BF16)
        for dy in range(3):
            for dx in range(3):
                rows = [grads[dx, pl.ds(dy * LANES + z, 32, stride=4), :] for z in range(4)]
                for dz in range(3):
                    total = jnp.zeros((32, LANES), F32)
                    for z in range(4):
                        if 0 <= z + 1 - dz < 4:
                            total = jnp.where(on_plane[z + 1 - dz], rows[z], total)
                    t = 9 * dz + 3 * dy + dx
                    terms[t // 4 * 32 : t // 4 * 32 + 32, t % 4 * LANES : (t % 4 + 1) * LANES] = total.astype(BF16)
        packed = jnp.dot(terms[...], collapse, preferred_element_type=F32).astype(BF16)
        wg_all[which, slot_of(s)] = packed

    for s in (3, 2, 1, 0):
        source = crop if s == 0 else feats.at[0] if s == 1 else merged.at[s - 2]
        low, high = 8 + 2 * (3 - s), 28 - 2 * (3 - s)

        def to_first(base, span, v, s=s):
            fd[pl.ds(base, span), :] = (v * slope(pre1[s, pl.ds(base, span), :])).astype(BF16)

        kernel_grads(hidden.at[s], sd, s, 1)
        conv(sd, wb.at[2 * s + 1], low + 1, high - 1, to_first)
        clear_outside(fd, low + 1, high - 1)
        kernel_grads(source, fd, s, 0)

        def to_delta(base, span, v, s=s):
            out = v.astype(BF16)
            if s == 1 or s == 0:
                other = delta[2 if s == 1 else 3, pl.ds(base, span), :]
                out = (out.astype(F32) + other.astype(F32)).astype(BF16)
            delta[s, pl.ds(base, span), :] = out
            if s > 0:
                sd[pl.ds(base, span), :] = (
                    out.astype(F32) * slope(pre2[s - 1, pl.ds(base, span), :])
                ).astype(BF16)

        conv(fd, wb.at[2 * s], low + 2, high - 2, to_delta)
        if s > 0:
            clear_outside(sd, low + 2, high - 2)

    for s in range(4):
        for y in range(ROWS):
            place = pl.ds(pl.multiple_of(base0 + y * WIDTH + own_low, 16), 64)
            out_all[slot_of(s), 64 * y : 64 * y + 64, :] = feats[s, place, :]
            out_all[slot_of(s), 256 + 64 * y : 320 + 64 * y, :] = delta[s, place, :]
    for k, out in enumerate((out0, out1, out2, out3)):
        out[...] = out_all[k]
    for k, keep in enumerate((keep0, keep1, keep2, keep3)):
        keep[...] = wg_all[core, k]
    send[...] = wg_all[1 - core]


VMEM = pl.BlockSpec(memory_space=pltpu.VMEM)
MATRICES = (8, 3 * LANES, 3 * LANES)


def build_call(*packs):
    return pl.pallas_call(
        build_kernel,
        out_shape=[jax.ShapeDtypeStruct(MATRICES, BF16)] * 2,
        in_specs=[VMEM] * 4,
        out_specs=[VMEM] * 2,
        scratch_shapes=[
            pltpu.VMEM((4, 2, 224, LANES), BF16),
            pltpu.VMEM((224, 4 * LANES), F32),
            pltpu.VMEM((7 * LANES, LANES), F32),
            pltpu.VMEM((2, LANES, LANES), F32),
        ],
        compiler_params=pltpu.CompilerParams(vmem_limit_bytes=8 * 1024 * 1024),
        cost_estimate=pl.CostEstimate(flops=5_000_000_000, bytes_accessed=10_000_000, transcendentals=0),
        name="banded",
    )(*packs)


def main_call(*operands):
    acts = (TOTAL * WIDTH, LANES)
    return pl.pallas_call(
        main_kernel,
        out_shape=[jax.ShapeDtypeStruct((512, LANES), BF16)] * 4
        + [jax.ShapeDtypeStruct((224, LANES), BF16)] * 4
        + [jax.ShapeDtypeStruct((4, 224, LANES), BF16)],
        in_specs=[VMEM] * 8,
        out_specs=[VMEM] * 9,
        scratch_shapes=[
            pltpu.VMEM(acts, BF16),
            pltpu.VMEM((20 * WIDTH, LANES), BF16),
            pltpu.VMEM((4,) + acts, BF16),
            pltpu.VMEM((2,) + acts, BF16),
            pltpu.VMEM((4,) + acts, BF16),
            pltpu.VMEM((4,) + acts, BF16),
            pltpu.VMEM(acts, BF16),
            pltpu.VMEM(acts, BF16),
            pltpu.VMEM((4,) + acts, F32),
            pltpu.VMEM((4,) + acts, F32),
            pltpu.VMEM((3, 3 * LANES, LANES), F32),
            pltpu.VMEM((224, 4 * LANES), BF16),
            pltpu.VMEM((4, 512, LANES), BF16),
            pltpu.VMEM((2, 4, 224, LANES), BF16),
        ],
        compiler_params=pltpu.CompilerParams(vmem_limit_bytes=40 * 1024 * 1024),
        cost_estimate=pl.CostEstimate(flops=20_000_000_000, bytes_accessed=10_000_000, transcendentals=0),
        name="sections",
    )(*operands)


def layout_kernel(in0, in1, in2, in3, features, gradients, by_source):
    seg = lax.axis_index("segment")
    for k, arrived in enumerate((in0, in1, in2, in3)):
        by_source[lax.rem(seg - k + 4, 4)] = arrived[...]
    for which, out in enumerate((features, gradients)):
        for m in range(2):
            planes = []
            for y in range(ROWS):
                start = 256 * which + 64 * y
                row = jnp.concatenate([by_source[m, start : start + 64, :], by_source[2 + m, start : start + 64, :]])
                planes.append(row.astype(F32).T[:, None, :])
            out[m] = jnp.concatenate(planes, axis=1).astype(out.dtype)


def layout_call(*arrived):
    return pl.pallas_call(
        layout_kernel,
        out_shape=[
            jax.ShapeDtypeStruct((2, LANES, ROWS, LANES), BF16),
            jax.ShapeDtypeStruct((2, LANES, ROWS, LANES), F32),
        ],
        in_specs=[VMEM] * 4,
        out_specs=[VMEM] * 2,
        scratch_shapes=[pltpu.VMEM((4, 512, LANES), BF16)],
        compiler_params=pltpu.CompilerParams(vmem_limit_bytes=8 * 1024 * 1024),
        cost_estimate=pl.CostEstimate(flops=4_000_000_000, bytes_accessed=4_000_000, transcendentals=0),
        name="layout",
    )(*arrived)


def rotated(value, axis, group, step, stride):
    count = lax.axis_size(axis)

    def target(i):
        place = i // stride % group
        return i + ((place + step) % group - place) * stride

    return lax.ppermute(value, axis, [(i, target(i)) for i in range(count)])


def local(crops, cotangent, weights):
    micro_count, channels, planes, rows, across = crops.shape
    seg = lax.axis_index("segment")
    micro, half = seg % 2, seg // 2
    devices = lax.axis_size("gy")
    swap = [(i, i ^ 1) for i in range(devices)]

    def tile(volume):
        field = lax.dynamic_index_in_dim(volume, micro, 0, keepdims=False)
        field = jnp.transpose(field, (2, 3, 0, 1)).reshape(rows, across, channels * planes)
        return lax.dynamic_slice_in_dim(field, half * 48, WIDTH, 1).reshape(rows * WIDTH, channels * planes)

    own = jnp.stack([tile(crops), tile(cotangent)])
    packed = jnp.pad(weights[0], ((0, 0), (0, 1), (0, 0), (0, 0))).reshape(2, 7, 4, channels, channels)
    packed = jnp.transpose(packed, (0, 1, 3, 2, 4)).reshape(2, 7 * channels, 4 * channels)

    others = [rotated(packed, "segment", 4, k, 1) for k in (1, 2, 3)]
    oth = lax.ppermute(own, "gy", swap)
    block = jnp.concatenate([own, oth], axis=1)

    def outward(distance):
        return [
            (i, i + 2 * distance * (1 if i % 2 == 0 else -1))
            for i in range(devices)
            if 0 <= i + 2 * distance * (1 if i % 2 == 0 else -1) < devices
        ]

    near = lax.ppermute(block, "gy", outward(1))
    far = lax.ppermute(block[0], "gy", outward(2))
    w1, wb = build_call(packed, *others)
    near, far, w1 = lax.optimization_barrier((near, far, w1))
    near_other = lax.ppermute(near, "gy", swap)
    far_other = lax.ppermute(far, "gy", swap)
    outs = main_call(own, oth, near, far, near_other, far_other, w1, wb)
    fields, keep, send = outs[:4], outs[4:8], outs[8]

    got = lax.ppermute(send, "gy", swap)
    part = [(keep[k].astype(F32) + got[k].astype(F32)).astype(BF16) for k in range(4)]
    total = part[0].astype(F32)
    for k in (1, 2, 3):
        total = total + rotated(part[k], "segment", 4, k, 1).astype(F32)
    arrived = [rotated(fields[k], "segment", 4, k, 1) for k in (1, 2, 3)]
    for stride in (2, 8):
        mine = total.astype(BF16)
        if stride == 2:
            mine, *arrived = lax.optimization_barrier((mine, *arrived))
        total = mine.astype(F32)
        for k in (1, 2, 3):
            total = total + rotated(mine, "gy", 4, k, stride).astype(F32)
    features, input_grads = layout_call(fields[0], *arrived)
    mine, features, input_grads = lax.optimization_barrier((total.astype(BF16), features, input_grads))
    other = lax.ppermute(mine, "gy", swap)
    low_core = lax.axis_index("gy") % 2 == 0
    both = jnp.stack([jnp.where(low_core, mine, other), jnp.where(low_core, other, mine)])
    grads = both.reshape(2, 7, channels, 4, channels).transpose(0, 1, 3, 2, 4)
    grads = grads.reshape(2, 28, channels, channels)[:, :27].astype(F32)

    shape = (1, micro_count, channels, planes, rows, across)
    return features.reshape(shape), grads[None], input_grads.reshape(shape)


def solution(mesh):
    return jax.shard_map(
        local,
        mesh=mesh,
        in_specs=(
            P(None, None, None, "gy", None),
            P(None, None, None, "gy", None),
            P("segment", None, None, None, None),
        ),
        out_specs=(
            P("segment", None, None, None, "gy", None),
            P("segment", None, None, None, None),
            P("segment", None, None, None, "gy", None),
        ),
        check_vma=False,
    )
```

```python
import jax
import jax.numpy as jnp
from jax import lax
from jax.experimental import pallas as pl
from jax.experimental.pallas import tpu as pltpu
from jax.sharding import PartitionSpec as P

ROWS = 4
WIDTH = 80
TOTAL = 36
LANES = 128
PAIRS = 4
F32 = jnp.float32
BF16 = jnp.bfloat16


def sigmoid(v):
    return 0.5 * jnp.tanh(0.5 * v) + 0.5


def slope(v):
    s = sigmoid(v)
    return s * (1.0 + v * (1.0 - s))


def at_row(row):
    return pl.multiple_of(row * WIDTH, 16)


def constants():
    er = lax.broadcasted_iota(jnp.int32, (LANES, 4 * LANES), 0)
    ec = lax.broadcasted_iota(jnp.int32, (LANES, 4 * LANES), 1)
    expand = jnp.where(er == lax.shift_right_logical(ec, 2), 1.0, 0.0).astype(BF16)
    cr = lax.broadcasted_iota(jnp.int32, (4 * LANES, LANES), 0)
    cc = lax.broadcasted_iota(jnp.int32, (4 * LANES, LANES), 1)
    collapse = jnp.where(cc == lax.shift_right_logical(cr, 2), 1.0, 0.0).astype(BF16)
    plane = lax.bitwise_and(lax.broadcasted_iota(jnp.int32, (32, LANES), 1), 3)
    return expand, collapse, [plane == z for z in range(4)]


def build_kernel(pack0, pack1, pack2, pack3, w1, wb, wpack, lx, lxt, block):
    seg = lax.axis_index("segment")
    for k, pack in enumerate((pack0, pack1, pack2, pack3)):
        wpack[lax.rem(seg - k + 4, 4)] = pack[...]
    expand, _, on_plane = constants()
    nothing = jnp.zeros((LANES, LANES), BF16)

    def place(dst, index, row, col, value):
        dst[index, row * LANES : (row + 1) * LANES, col * LANES : (col + 1) * LANES] = value

    def build(index, carry):
        for dx in range(3):
            for dst in (w1, wb):
                place(dst, index, 3, dx, nothing)
                place(dst, index, 0, 3 + dx, nothing)
        w = wpack[lax.div(index, 2), lax.rem(index, 2)]
        lx[...] = jnp.dot(w, expand, preferred_element_type=F32)
        for q in range(7):
            lxt[q * LANES : (q + 1) * LANES, :] = lax.dot_general(
                w[q * 32 : (q + 1) * 32], expand[:32, :LANES], (((0,), (0,)), ((), ())), preferred_element_type=F32
            )
        for dy in range(3):
            for dx in range(3):
                taps = [9 * dz + 3 * dy + dx for dz in range(3)]
                fwd = [lx[t // 4 * 32 : t // 4 * 32 + 32, t % 4 * LANES : (t % 4 + 1) * LANES] for t in taps]
                bwd = [lxt[t * 32 : t * 32 + 32, :] for t in taps]
                for z in range(4):
                    vf = jnp.zeros((32, LANES), F32)
                    vb = jnp.zeros((32, LANES), F32)
                    for dz in range(3):
                        if 0 <= z + 1 - dz < 4:
                            vf = jnp.where(on_plane[z + 1 - dz], fwd[dz], vf)
                        if 0 <= z + dz - 1 < 4:
                            vb = jnp.where(on_plane[z + dz - 1], bwd[dz], vb)
                    block[6 * dy + 2 * dx, pl.ds(z, 32, stride=4), :] = vf
                    block[6 * dy + 2 * dx + 1, pl.ds(z, 32, stride=4), :] = vb
        for dy in range(3):
            for dx in range(3):
                ahead = block[6 * dy + 2 * dx].astype(BF16)
                back = block[6 * dy + 2 * dx + 1].astype(BF16)
                for r in range(2):
                    place(w1, index, dy + r, 3 * r + dx, ahead)
                    place(wb, index, 2 - dy + r, 3 * r + 2 - dx, back)
        return carry

    lax.fori_loop(0, 8, build, 0)


def main_kernel(
    own, oth, near, far, near_other, far_other, w1, wb,
    out0, out1, out2, out3, keep0, keep1, keep2, keep3, send,
    crop, cot, feats, merged, hidden, delta, sd, fd, pre1, pre2, product, grads, terms, out_all, wg_all,
):
    seg = lax.axis_index("segment")
    gy = lax.axis_index("gy")
    core = lax.rem(gy, 2)
    half = lax.div(seg, 2)
    column = lax.broadcasted_iota(jnp.int32, (1, WIDTH, LANES), 1)

    def put(dst, row, src, src_row, rows):
        dst[row * WIDTH : (row + rows) * WIDTH, :] = src[src_row * WIDTH : (src_row + rows) * WIDTH, :]

    @pl.when(core == 0)
    def _():
        put(crop, 0, far, 0, 8)
        put(crop, 8, near.at[0], 0, 8)
        put(crop, 16, own.at[0], 0, 4)
        put(crop, 20, oth.at[0], 0, 4)
        put(crop, 24, near_other.at[0], 4, 4)
        put(crop, 28, near_other.at[0], 0, 4)
        put(crop, 32, far_other, 4, 4)
        put(cot, 0, near.at[1], 0, 8)
        put(cot, 8, own.at[1], 0, 4)
        put(cot, 12, oth.at[1], 0, 4)
        put(cot, 16, near_other.at[1], 4, 4)

    @pl.when(core == 1)
    def _():
        put(crop, 0, far_other, 4, 4)
        put(crop, 4, near_other.at[0], 0, 8)
        put(crop, 12, oth.at[0], 0, 4)
        put(crop, 16, own.at[0], 0, 4)
        put(crop, 20, near.at[0], 4, 4)
        put(crop, 24, near.at[0], 0, 4)
        put(crop, 28, far, 4, 4)
        put(crop, 32, far, 0, 4)
        put(cot, 0, near_other.at[1], 4, 4)
        put(cot, 4, oth.at[1], 0, 4)
        put(cot, 8, own.at[1], 0, 4)
        put(cot, 12, near.at[1], 4, 4)
        put(cot, 16, near.at[1], 0, 4)

    _, collapse, on_plane = constants()

    def by_rows(v):
        return v.reshape(v.shape[0] // WIDTH, WIDTH, LANES)

    def from_left(v):
        return jnp.where(column == 0, 0.0, pltpu.roll(by_rows(v), 1, 1)).reshape(v.shape)

    def from_right(v):
        return jnp.where(column == WIDTH - 1, 0.0, pltpu.roll(by_rows(v), WIDTH - 1, 1)).reshape(v.shape)

    def stacked(src, first_rows, count):
        return jnp.concatenate(
            [
                jnp.concatenate([src[(row + j) * WIDTH : (row + j + 1) * WIDTH, :] for row in first_rows], axis=0)
                for j in range(count)
            ],
            axis=1,
        )

    def conv(src, matrix, low, high, then):
        rows = range(low, high, 2)
        for at in range(0, len(rows), PAIRS):
            some = rows[at : at + PAIRS]
            product[at * WIDTH : (at + len(some)) * WIDTH, :] = jnp.dot(
                stacked(src, [row - 1 for row in some], 4), matrix[...], preferred_element_type=F32
            )

            def finish(i, row):
                for r in range(2):
                    block = product.at[i * WIDTH : (i + 1) * WIDTH]
                    q = [block[:, (3 * r + b) * LANES : (3 * r + b + 1) * LANES] for b in range(3)]
                    here = slice((row + r) * WIDTH, (row + r + 1) * WIDTH)
                    then(here, q[1] + from_left(q[0]) + from_right(q[2]))

            for i, row in enumerate(some):
                finish(at + i, row)

    def clear_outside(dst, low, high, first=16):
        top = first - ROWS * gy
        bottom = first + ROWS * (lax.axis_size("gy") - gy)

        def clear(i, carry):
            dst[pl.ds(at_row(i), WIDTH), :] = jnp.zeros((WIDTH, LANES), BF16)
            return carry

        @pl.when(top > low)
        def _():
            lax.fori_loop(low, jnp.minimum(top, high), clear, 0)

        @pl.when(bottom < high)
        def _():
            lax.fori_loop(jnp.maximum(bottom, low), high, clear, 0)

    clear_outside(crop, 0, 36)
    clear_outside(cot, 0, 20, 8)

    for s in range(4):
        source = crop if s == 0 else feats.at[0] if s == 1 else merged.at[s - 2]

        def first(here, v, s=s):
            pre1[s, here, :] = v
            hidden[s, here, :] = (v * sigmoid(v)).astype(BF16)

        conv(source, w1.at[2 * s], 2 * s + 1, 35 - 2 * s, first)
        clear_outside(hidden.at[s], 2 * s + 1, 35 - 2 * s)

        def second(here, v, s=s):
            pre2[s, here, :] = v
            out = (v * sigmoid(v)).astype(BF16)
            feats[s, here, :] = out
            if s == 1 or s == 2:
                skip = feats[0, here, :] if s == 1 else crop[here, :]
                merged[s - 1, here, :] = (out.astype(F32) + skip.astype(F32)).astype(BF16)

        conv(hidden.at[s], w1.at[2 * s + 1], 2 * s + 2, 34 - 2 * s, second)
        if s == 0:
            clear_outside(feats.at[0], 2, 34)
        if s == 1 or s == 2:
            clear_outside(merged.at[s - 1], 2 * s + 2, 34 - 2 * s)

    here = slice(8 * WIDTH, 28 * WIDTH)
    sd[here, :] = (cot[...].astype(F32) * slope(pre2[3, here, :])).astype(BF16)

    own_low = half * 16
    mine = (column >= own_low) & (column < own_low + 64)
    base0 = 16 * WIDTH
    span = ROWS * WIDTH
    slot_of = lambda s: lax.rem(s - seg + 4, 4)

    def kernel_grads(src, grad, s, which):
        d = jnp.where(mine, by_rows(grad[base0 : base0 + span, :].astype(F32)), 0.0).reshape(span, LANES)
        shifted = jnp.concatenate([from_right(d).astype(BF16), d.astype(BF16), from_left(d).astype(BF16)], axis=1)
        product = lax.dot_general(
            stacked(src, range(15, 19), 3), shifted, (((0,), (0,)), ((), ())), preferred_element_type=F32
        )
        for dx in range(3):
            grads[dx] = product[:, dx * LANES : (dx + 1) * LANES]
        terms[6 * 32 :, 3 * LANES :] = jnp.zeros((32, LANES), BF16)
        for dy in range(3):
            for dx in range(3):
                rows = [grads[dx, pl.ds(dy * LANES + z, 32, stride=4), :] for z in range(4)]
                for dz in range(3):
                    total = jnp.zeros((32, LANES), F32)
                    for z in range(4):
                        if 0 <= z + 1 - dz < 4:
                            total = jnp.where(on_plane[z + 1 - dz], rows[z], total)
                    t = 9 * dz + 3 * dy + dx
                    terms[t // 4 * 32 : t // 4 * 32 + 32, t % 4 * LANES : (t % 4 + 1) * LANES] = total.astype(BF16)
        packed = jnp.dot(terms[...], collapse, preferred_element_type=F32).astype(BF16)
        wg_all[which, slot_of(s)] = packed

    for s in (3, 2, 1, 0):
        source = crop if s == 0 else feats.at[0] if s == 1 else merged.at[s - 2]
        low, high = 8 + 2 * (3 - s), 28 - 2 * (3 - s)

        def to_first(here, v, s=s):
            fd[here, :] = (v * slope(pre1[s, here, :])).astype(BF16)

        kernel_grads(hidden.at[s], sd, s, 1)
        conv(sd, wb.at[2 * s + 1], low + 1, high - 1, to_first)
        clear_outside(fd, low + 1, high - 1)
        kernel_grads(source, fd, s, 0)

        def to_delta(here, v, s=s):
            out = v.astype(BF16)
            if s == 1 or s == 0:
                other = delta[2 if s == 1 else 3, here, :]
                out = (out.astype(F32) + other.astype(F32)).astype(BF16)
            delta[s, here, :] = out
            if s > 0:
                sd[here, :] = (
                    out.astype(F32) * slope(pre2[s - 1, here, :])
                ).astype(BF16)

        conv(fd, wb.at[2 * s], low + 2, high - 2, to_delta)
        if s > 0:
            clear_outside(sd, low + 2, high - 2)

    for s in range(4):
        for y in range(ROWS):
            place = pl.ds(pl.multiple_of(base0 + y * WIDTH + own_low, 16), 64)
            out_all[slot_of(s), 64 * y : 64 * y + 64, :] = feats[s, place, :]
            out_all[slot_of(s), 256 + 64 * y : 320 + 64 * y, :] = delta[s, place, :]
    for k, out in enumerate((out0, out1, out2, out3)):
        out[...] = out_all[k]
    for k, keep in enumerate((keep0, keep1, keep2, keep3)):
        keep[...] = wg_all[core, k]
    send[...] = wg_all[1 - core]


VMEM = pl.BlockSpec(memory_space=pltpu.VMEM)
MATRICES = (8, 4 * LANES, 6 * LANES)


def build_call(*packs):
    return pl.pallas_call(
        build_kernel,
        out_shape=[jax.ShapeDtypeStruct(MATRICES, BF16)] * 2,
        in_specs=[VMEM] * 4,
        out_specs=[VMEM] * 2,
        scratch_shapes=[
            pltpu.VMEM((4, 2, 224, LANES), BF16),
            pltpu.VMEM((224, 4 * LANES), F32),
            pltpu.VMEM((7 * LANES, LANES), F32),
            pltpu.VMEM((18, LANES, LANES), F32),
        ],
        compiler_params=pltpu.CompilerParams(vmem_limit_bytes=8 * 1024 * 1024),
        cost_estimate=pl.CostEstimate(flops=5_000_000_000, bytes_accessed=10_000_000, transcendentals=0),
        name="banded",
    )(*packs)


def main_call(*operands):
    acts = (TOTAL * WIDTH, LANES)
    return pl.pallas_call(
        main_kernel,
        out_shape=[jax.ShapeDtypeStruct((512, LANES), BF16)] * 4
        + [jax.ShapeDtypeStruct((224, LANES), BF16)] * 4
        + [jax.ShapeDtypeStruct((4, 224, LANES), BF16)],
        in_specs=[VMEM] * 8,
        out_specs=[VMEM] * 9,
        scratch_shapes=[
            pltpu.VMEM(acts, BF16),
            pltpu.VMEM((20 * WIDTH, LANES), BF16),
            pltpu.VMEM((4,) + acts, BF16),
            pltpu.VMEM((2,) + acts, BF16),
            pltpu.VMEM((4,) + acts, BF16),
            pltpu.VMEM((4,) + acts, BF16),
            pltpu.VMEM(acts, BF16),
            pltpu.VMEM(acts, BF16),
            pltpu.VMEM((4,) + acts, F32),
            pltpu.VMEM((4,) + acts, F32),
            pltpu.VMEM((17 * WIDTH, 6 * LANES), F32),
            pltpu.VMEM((3, 3 * LANES, LANES), F32),
            pltpu.VMEM((224, 4 * LANES), BF16),
            pltpu.VMEM((4, 512, LANES), BF16),
            pltpu.VMEM((2, 4, 224, LANES), BF16),
        ],
        compiler_params=pltpu.CompilerParams(vmem_limit_bytes=36 * 1024 * 1024),
        cost_estimate=pl.CostEstimate(flops=20_000_000_000, bytes_accessed=10_000_000, transcendentals=0),
        name="sections",
    )(*operands)


def layout_kernel(in0, in1, in2, in3, features, gradients, by_source):
    seg = lax.axis_index("segment")
    for k, arrived in enumerate((in0, in1, in2, in3)):
        by_source[lax.rem(seg - k + 4, 4)] = arrived[...]
    for which, out in enumerate((features, gradients)):
        for m in range(2):
            planes = []
            for y in range(ROWS):
                start = 256 * which + 64 * y
                row = jnp.concatenate([by_source[m, start : start + 64, :], by_source[2 + m, start : start + 64, :]])
                planes.append(row.astype(F32).T[:, None, :])
            out[m] = jnp.concatenate(planes, axis=1).astype(out.dtype)


def layout_call(*arrived):
    return pl.pallas_call(
        layout_kernel,
        out_shape=[
            jax.ShapeDtypeStruct((2, LANES, ROWS, LANES), BF16),
            jax.ShapeDtypeStruct((2, LANES, ROWS, LANES), F32),
        ],
        in_specs=[VMEM] * 4,
        out_specs=[VMEM] * 2,
        scratch_shapes=[pltpu.VMEM((4, 512, LANES), BF16)],
        compiler_params=pltpu.CompilerParams(vmem_limit_bytes=8 * 1024 * 1024),
        cost_estimate=pl.CostEstimate(flops=4_000_000_000, bytes_accessed=4_000_000, transcendentals=0),
        name="layout",
    )(*arrived)


def rotated(value, axis, group, step, stride):
    count = lax.axis_size(axis)

    def target(i):
        place = i // stride % group
        return i + ((place + step) % group - place) * stride

    return lax.ppermute(value, axis, [(i, target(i)) for i in range(count)])


def local(crops, cotangent, weights):
    micro_count, channels, planes, rows, across = crops.shape
    seg = lax.axis_index("segment")
    micro, half = seg % 2, seg // 2
    devices = lax.axis_size("gy")
    swap = [(i, i ^ 1) for i in range(devices)]

    def tile(volume):
        field = lax.dynamic_index_in_dim(volume, micro, 0, keepdims=False)
        field = jnp.transpose(field, (2, 3, 0, 1)).reshape(rows, across, channels * planes)
        return lax.dynamic_slice_in_dim(field, half * 48, WIDTH, 1).reshape(rows * WIDTH, channels * planes)

    own = jnp.stack([tile(crops), tile(cotangent)])
    packed = jnp.pad(weights[0], ((0, 0), (0, 1), (0, 0), (0, 0))).reshape(2, 7, 4, channels, channels)
    packed = jnp.transpose(packed, (0, 1, 3, 2, 4)).reshape(2, 7 * channels, 4 * channels)

    others = [rotated(packed, "segment", 4, k, 1) for k in (1, 2, 3)]
    oth = lax.ppermute(own, "gy", swap)
    block = jnp.concatenate([own, oth], axis=1)

    def outward(distance):
        return [(i, (i + 2 * distance * (1 if i % 2 == 0 else -1)) % devices) for i in range(devices)]

    near = lax.ppermute(block, "gy", outward(1))
    far = lax.ppermute(block[0], "gy", outward(2))
    w1, wb = build_call(packed, *others)
    near, far, w1 = lax.optimization_barrier((near, far, w1))
    near_other = lax.ppermute(near, "gy", swap)
    far_other = lax.ppermute(far, "gy", swap)
    outs = main_call(own, oth, near, far, near_other, far_other, w1, wb)
    fields, keep, send = outs[:4], outs[4:8], outs[8]

    got = lax.ppermute(send, "gy", swap)
    part = [(keep[k].astype(F32) + got[k].astype(F32)).astype(BF16) for k in range(4)]
    total = part[0].astype(F32)
    for k in (1, 2, 3):
        total = total + rotated(part[k], "segment", 4, k, 1).astype(F32)
    arrived = [rotated(fields[k], "segment", 4, k, 1) for k in (1, 2, 3)]
    for stride in (2, 8):
        mine = total.astype(BF16)
        if stride == 2:
            mine, *arrived = lax.optimization_barrier((mine, *arrived))
        total = mine.astype(F32)
        for k in (1, 2, 3):
            total = total + rotated(mine, "gy", 4, k, stride).astype(F32)
    features, input_grads = layout_call(fields[0], *arrived)
    mine, features, input_grads = lax.optimization_barrier((total.astype(BF16), features, input_grads))
    other = lax.ppermute(mine, "gy", swap)
    low_core = lax.axis_index("gy") % 2 == 0
    both = jnp.stack([jnp.where(low_core, mine, other), jnp.where(low_core, other, mine)])
    grads = both.reshape(2, 7, channels, 4, channels).transpose(0, 1, 3, 2, 4)
    grads = grads.reshape(2, 28, channels, channels)[:, :27].astype(F32)

    shape = (1, micro_count, channels, planes, rows, across)
    return features.reshape(shape), grads[None], input_grads.reshape(shape)


def solution(mesh):
    return jax.shard_map(
        local,
        mesh=mesh,
        in_specs=(
            P(None, None, None, "gy", None),
            P(None, None, None, "gy", None),
            P("segment", None, None, None, None),
        ),
        out_specs=(
            P("segment", None, None, None, "gy", None),
            P("segment", None, None, None, None),
            P("segment", None, None, None, "gy", None),
        ),
        check_vma=False,
    )
```

```python
import jax
import jax.numpy as jnp
from jax import lax
from jax.experimental import pallas as pl
from jax.experimental.pallas import tpu as pltpu
from jax.sharding import PartitionSpec as P

ROWS = 4
WIDTH = 80
TOTAL = 36
LANES = 128
PAIRS = 4
F32 = jnp.float32
BF16 = jnp.bfloat16


def sigmoid(v):
    return 0.5 * jnp.tanh(0.5 * v) + 0.5


def slope(v):
    s = sigmoid(v)
    return s * (1.0 + v * (1.0 - s))


def at_row(row):
    return pl.multiple_of(row * WIDTH, 16)


def grouped(i):
    return lax.shift_right_logical(i, 7) * 32 + lax.bitwise_and(i, 31)


def constants():
    er = lax.broadcasted_iota(jnp.int32, (LANES, 4 * LANES), 0)
    ec = lax.broadcasted_iota(jnp.int32, (LANES, 4 * LANES), 1)
    expand = jnp.where(er == grouped(ec), 1.0, 0.0).astype(BF16)
    cr = lax.broadcasted_iota(jnp.int32, (4 * LANES, LANES), 0)
    cc = lax.broadcasted_iota(jnp.int32, (4 * LANES, LANES), 1)
    collapse = jnp.where(cc == grouped(cr), 1.0, 0.0).astype(BF16)
    plane = lax.shift_right_logical(lax.broadcasted_iota(jnp.int32, (32, LANES), 1), 5)
    return expand, collapse, [plane == z for z in range(4)]


def build_kernel(pack0, pack1, pack2, pack3, w1, wb, wpack, lx, lxt):
    seg = lax.axis_index("segment")
    for k, pack in enumerate((pack0, pack1, pack2, pack3)):
        wpack[lax.rem(seg - k + 4, 4)] = pack[...]
    expand, _, on_plane = constants()
    nothing = jnp.zeros((32, LANES), BF16)

    def place(dst, index, row, col, value):
        dst[index, row * 32 : (row + 1) * 32, col * LANES : (col + 1) * LANES] = value

    def build(index, carry):
        for dx in range(3):
            for dst in (w1, wb):
                for z in range(4):
                    place(dst, index, 12 + z, dx, nothing)
                    place(dst, index, z, 3 + dx, nothing)
        w = wpack[lax.div(index, 2), lax.rem(index, 2)]
        lx[...] = jnp.dot(w, expand, preferred_element_type=F32)
        for q in range(7):
            lxt[q * LANES : (q + 1) * LANES, :] = lax.dot_general(
                w[q * 32 : (q + 1) * 32], expand[:32, :LANES], (((0,), (0,)), ((), ())), preferred_element_type=F32
            )
        for dy in range(3):
            for dx in range(3):
                taps = [9 * dz + 3 * dy + dx for dz in range(3)]
                fwd = [lx[t // 4 * 32 : t // 4 * 32 + 32, t % 4 * LANES : (t % 4 + 1) * LANES] for t in taps]
                bwd = [lxt[t * 32 : t * 32 + 32, :] for t in taps]
                for z in range(4):
                    vf = jnp.zeros((32, LANES), F32)
                    vb = jnp.zeros((32, LANES), F32)
                    for dz in range(3):
                        if 0 <= z + 1 - dz < 4:
                            vf = jnp.where(on_plane[z + 1 - dz], fwd[dz], vf)
                        if 0 <= z + dz - 1 < 4:
                            vb = jnp.where(on_plane[z + dz - 1], bwd[dz], vb)
                    for r in range(2):
                        place(w1, index, 4 * (dy + r) + z, 3 * r + dx, vf.astype(BF16))
                        place(wb, index, 4 * (2 - dy + r) + z, 3 * r + 2 - dx, vb.astype(BF16))
        return carry

    lax.fori_loop(0, 8, build, 0)


def by_rows(v):
    return v.reshape(v.shape[0] // WIDTH, WIDTH, LANES)


def from_left(v):
    column = lax.broadcasted_iota(jnp.int32, (1, WIDTH, LANES), 1)
    return jnp.where(column == 0, 0.0, pltpu.roll(by_rows(v), 1, 1)).reshape(v.shape)


def from_right(v):
    column = lax.broadcasted_iota(jnp.int32, (1, WIDTH, LANES), 1)
    return jnp.where(column == WIDTH - 1, 0.0, pltpu.roll(by_rows(v), WIDTH - 1, 1)).reshape(v.shape)


def stacked(src, first_rows, count):
    return jnp.concatenate(
        [
            jnp.concatenate([src[(row + j) * WIDTH : (row + j + 1) * WIDTH, :] for row in first_rows], axis=0)
            for j in range(count)
        ],
        axis=1,
    )


def main_kernel(
    own, oth, near, far, near_other, far_other, w1, wb,
    out0, out1, out2, out3, windows, deltas,
    crop, cot, feats, merged, hidden, delta, sd, fd, pre1, pre2, product, out_all,
):
    seg = lax.axis_index("segment")
    gy = lax.axis_index("gy")
    core = lax.rem(gy, 2)
    half = lax.div(seg, 2)
    column = lax.broadcasted_iota(jnp.int32, (1, WIDTH, LANES), 1)

    def put(dst, row, src, src_row, rows):
        dst[row * WIDTH : (row + rows) * WIDTH, :] = src[src_row * WIDTH : (src_row + rows) * WIDTH, :]

    @pl.when(core == 0)
    def _():
        put(crop, 0, far, 0, 8)
        put(crop, 8, near.at[0], 0, 8)
        put(crop, 16, own.at[0], 0, 4)
        put(crop, 20, oth.at[0], 0, 4)
        put(crop, 24, near_other.at[0], 4, 4)
        put(crop, 28, near_other.at[0], 0, 4)
        put(crop, 32, far_other, 4, 4)
        put(cot, 0, near.at[1], 0, 8)
        put(cot, 8, own.at[1], 0, 4)
        put(cot, 12, oth.at[1], 0, 4)
        put(cot, 16, near_other.at[1], 4, 4)

    @pl.when(core == 1)
    def _():
        put(crop, 0, far_other, 4, 4)
        put(crop, 4, near_other.at[0], 0, 8)
        put(crop, 12, oth.at[0], 0, 4)
        put(crop, 16, own.at[0], 0, 4)
        put(crop, 20, near.at[0], 4, 4)
        put(crop, 24, near.at[0], 0, 4)
        put(crop, 28, far, 4, 4)
        put(crop, 32, far, 0, 4)
        put(cot, 0, near_other.at[1], 4, 4)
        put(cot, 4, oth.at[1], 0, 4)
        put(cot, 8, own.at[1], 0, 4)
        put(cot, 12, near.at[1], 4, 4)
        put(cot, 16, near.at[1], 0, 4)

    def conv(src, matrix, low, high, then):
        rows = range(low, high, 2)
        for at in range(0, len(rows), PAIRS):
            some = rows[at : at + PAIRS]
            product[at * WIDTH : (at + len(some)) * WIDTH, :] = jnp.dot(
                stacked(src, [row - 1 for row in some], 4), matrix[...], preferred_element_type=F32
            )

            def finish(i, row):
                for r in range(2):
                    block = product.at[i * WIDTH : (i + 1) * WIDTH]
                    q = [block[:, (3 * r + b) * LANES : (3 * r + b + 1) * LANES] for b in range(3)]
                    here = slice((row + r) * WIDTH, (row + r + 1) * WIDTH)
                    then(here, q[1] + from_left(q[0]) + from_right(q[2]))

            for i, row in enumerate(some):
                finish(at + i, row)

    def clear_outside(dst, low, high, first=16):
        top = first - ROWS * gy
        bottom = first + ROWS * (lax.axis_size("gy") - gy)

        def clear(i, carry):
            dst[pl.ds(at_row(i), WIDTH), :] = jnp.zeros((WIDTH, LANES), BF16)
            return carry

        @pl.when(top > low)
        def _():
            lax.fori_loop(low, jnp.minimum(top, high), clear, 0)

        @pl.when(bottom < high)
        def _():
            lax.fori_loop(jnp.maximum(bottom, low), high, clear, 0)

    clear_outside(crop, 0, 36)
    clear_outside(cot, 0, 20, 8)

    for s in range(4):
        source = crop if s == 0 else feats.at[0] if s == 1 else merged.at[s - 2]

        def first(here, v, s=s):
            pre1[s, here, :] = v
            hidden[s, here, :] = (v * sigmoid(v)).astype(BF16)

        conv(source, w1.at[2 * s], 2 * s + 1, 35 - 2 * s, first)
        clear_outside(hidden.at[s], 2 * s + 1, 35 - 2 * s)

        def second(here, v, s=s):
            pre2[s, here, :] = v
            out = (v * sigmoid(v)).astype(BF16)
            feats[s, here, :] = out
            if s == 1 or s == 2:
                skip = feats[0, here, :] if s == 1 else crop[here, :]
                merged[s - 1, here, :] = (out.astype(F32) + skip.astype(F32)).astype(BF16)

        conv(hidden.at[s], w1.at[2 * s + 1], 2 * s + 2, 34 - 2 * s, second)
        if s == 0:
            clear_outside(feats.at[0], 2, 34)
        if s == 1 or s == 2:
            clear_outside(merged.at[s - 1], 2 * s + 2, 34 - 2 * s)

    here = slice(8 * WIDTH, 28 * WIDTH)
    sd[here, :] = (cot[...].astype(F32) * slope(pre2[3, here, :])).astype(BF16)

    own_low = half * 16
    base0 = 16 * WIDTH
    slot_of = lambda s: lax.rem(s - seg + 4, 4)

    def keep(index, src, grad):
        windows[index] = src[15 * WIDTH : 21 * WIDTH, :]
        deltas[index] = grad[16 * WIDTH : 20 * WIDTH, :]

    for s in (3, 2, 1, 0):
        source = crop if s == 0 else feats.at[0] if s == 1 else merged.at[s - 2]
        low, high = 8 + 2 * (3 - s), 28 - 2 * (3 - s)

        def to_first(here, v, s=s):
            fd[here, :] = (v * slope(pre1[s, here, :])).astype(BF16)

        keep(2 * s + 1, hidden.at[s], sd)
        conv(sd, wb.at[2 * s + 1], low + 1, high - 1, to_first)
        clear_outside(fd, low + 1, high - 1)
        keep(2 * s, source, fd)

        def to_delta(here, v, s=s):
            out = v.astype(BF16)
            if s == 1 or s == 0:
                other = delta[2 if s == 1 else 3, here, :]
                out = (out.astype(F32) + other.astype(F32)).astype(BF16)
            delta[s, here, :] = out
            if s > 0:
                sd[here, :] = (
                    out.astype(F32) * slope(pre2[s - 1, here, :])
                ).astype(BF16)

        conv(fd, wb.at[2 * s], low + 2, high - 2, to_delta)
        if s > 0:
            clear_outside(sd, low + 2, high - 2)

    for s in range(4):
        for y in range(ROWS):
            place = pl.ds(pl.multiple_of(base0 + y * WIDTH + own_low, 16), 64)
            out_all[slot_of(s), 64 * y : 64 * y + 64, :] = feats[s, place, :]
            out_all[slot_of(s), 256 + 64 * y : 320 + 64 * y, :] = delta[s, place, :]
    for k, out in enumerate((out0, out1, out2, out3)):
        out[...] = out_all[k]


def grads_kernel(windows, deltas, keep0, keep1, keep2, keep3, send, grads, terms, wg_all):
    seg = lax.axis_index("segment")
    core = lax.rem(lax.axis_index("gy"), 2)
    own_low = lax.div(seg, 2) * 16
    column = lax.broadcasted_iota(jnp.int32, (1, WIDTH, LANES), 1)
    mine = (column >= own_low) & (column < own_low + 64)
    _, collapse, on_plane = constants()
    for index in range(8):
        d = jnp.where(mine, by_rows(deltas[index].astype(F32)), 0.0).reshape(ROWS * WIDTH, LANES)
        shifted = jnp.concatenate([from_right(d).astype(BF16), d.astype(BF16), from_left(d).astype(BF16)], axis=1)
        product = lax.dot_general(
            stacked(windows.at[index], range(ROWS), 3), shifted, (((0,), (0,)), ((), ())), preferred_element_type=F32
        )
        for dx in range(3):
            grads[index, dx] = product[:, dx * LANES : (dx + 1) * LANES]
        top = 224 * index
        terms[top + 6 * 32 : top + 7 * 32, 3 * LANES :] = jnp.zeros((32, LANES), BF16)
        for dy in range(3):
            for dx in range(3):
                first = [dy * LANES + z * 32 for z in range(4)]
                rows = [grads[index, dx, at : at + 32, :] for at in first]
                for dz in range(3):
                    total = jnp.zeros((32, LANES), F32)
                    for z in range(4):
                        if 0 <= z + 1 - dz < 4:
                            total = jnp.where(on_plane[z + 1 - dz], rows[z], total)
                    t = 9 * dz + 3 * dy + dx
                    at = top + t // 4 * 32
                    terms[at : at + 32, t % 4 * LANES : (t % 4 + 1) * LANES] = total.astype(BF16)
    packed = jnp.dot(terms[...], collapse, preferred_element_type=F32).astype(BF16)
    for s in range(4):
        for which in range(2):
            top = 224 * (2 * s + which)
            wg_all[which, lax.rem(s - seg + 4, 4)] = packed[top : top + 224]
    for k, keep in enumerate((keep0, keep1, keep2, keep3)):
        keep[...] = wg_all[core, k]
    send[...] = wg_all[1 - core]


VMEM = pl.BlockSpec(memory_space=pltpu.VMEM)
MATRICES = (8, 4 * LANES, 6 * LANES)


def build_call(*packs):
    return pl.pallas_call(
        build_kernel,
        out_shape=[jax.ShapeDtypeStruct(MATRICES, BF16)] * 2,
        in_specs=[VMEM] * 4,
        out_specs=[VMEM] * 2,
        scratch_shapes=[
            pltpu.VMEM((4, 2, 224, LANES), BF16),
            pltpu.VMEM((224, 4 * LANES), F32),
            pltpu.VMEM((7 * LANES, LANES), F32),
        ],
        compiler_params=pltpu.CompilerParams(vmem_limit_bytes=8 * 1024 * 1024),
        cost_estimate=pl.CostEstimate(flops=5_000_000_000, bytes_accessed=10_000_000, transcendentals=0),
        name="banded",
    )(*packs)


def main_call(*operands):
    acts = (TOTAL * WIDTH, LANES)
    return pl.pallas_call(
        main_kernel,
        out_shape=[jax.ShapeDtypeStruct((512, LANES), BF16)] * 4
        + [
            jax.ShapeDtypeStruct((8, 6 * WIDTH, LANES), BF16),
            jax.ShapeDtypeStruct((8, 4 * WIDTH, LANES), BF16),
        ],
        in_specs=[VMEM] * 8,
        out_specs=[VMEM] * 6,
        scratch_shapes=[
            pltpu.VMEM(acts, BF16),
            pltpu.VMEM((20 * WIDTH, LANES), BF16),
            pltpu.VMEM((4,) + acts, BF16),
            pltpu.VMEM((2,) + acts, BF16),
            pltpu.VMEM((4,) + acts, BF16),
            pltpu.VMEM((4,) + acts, BF16),
            pltpu.VMEM(acts, BF16),
            pltpu.VMEM(acts, BF16),
            pltpu.VMEM((4,) + acts, F32),
            pltpu.VMEM((4,) + acts, F32),
            pltpu.VMEM((17 * WIDTH, 6 * LANES), F32),
            pltpu.VMEM((4, 512, LANES), BF16),
        ],
        compiler_params=pltpu.CompilerParams(vmem_limit_bytes=36 * 1024 * 1024),
        cost_estimate=pl.CostEstimate(flops=20_000_000_000, bytes_accessed=10_000_000, transcendentals=0),
        name="sections",
    )(*operands)


def grads_call(windows, deltas):
    return pl.pallas_call(
        grads_kernel,
        out_shape=[jax.ShapeDtypeStruct((224, LANES), BF16)] * 4 + [jax.ShapeDtypeStruct((4, 224, LANES), BF16)],
        in_specs=[VMEM] * 2,
        out_specs=[VMEM] * 5,
        scratch_shapes=[
            pltpu.VMEM((8, 3, 3 * LANES, LANES), F32),
            pltpu.VMEM((8 * 224, 4 * LANES), BF16),
            pltpu.VMEM((2, 4, 224, LANES), BF16),
        ],
        compiler_params=pltpu.CompilerParams(vmem_limit_bytes=16 * 1024 * 1024),
        cost_estimate=pl.CostEstimate(flops=6_000_000_000, bytes_accessed=4_000_000, transcendentals=0),
        name="kernel_grads",
    )(windows, deltas)


def layout_kernel(in0, in1, in2, in3, features, gradients, by_source):
    seg = lax.axis_index("segment")
    for k, arrived in enumerate((in0, in1, in2, in3)):
        by_source[lax.rem(seg - k + 4, 4)] = arrived[...]
    for which, out in enumerate((features, gradients)):
        for m in range(2):
            planes = []
            for y in range(ROWS):
                start = 256 * which + 64 * y
                row = jnp.concatenate([by_source[m, start : start + 64, :], by_source[2 + m, start : start + 64, :]])
                planes.append(row.astype(F32).T[:, None, :])
            for z in range(4):
                part = [plane[32 * z : 32 * z + 32] for plane in planes]
                out[m, :, z] = jnp.concatenate(part, axis=1).astype(out.dtype)


def layout_call(*arrived):
    return pl.pallas_call(
        layout_kernel,
        out_shape=[
            jax.ShapeDtypeStruct((2, 32, 4, ROWS, LANES), BF16),
            jax.ShapeDtypeStruct((2, 32, 4, ROWS, LANES), F32),
        ],
        in_specs=[VMEM] * 4,
        out_specs=[VMEM] * 2,
        scratch_shapes=[pltpu.VMEM((4, 512, LANES), BF16)],
        compiler_params=pltpu.CompilerParams(vmem_limit_bytes=8 * 1024 * 1024),
        cost_estimate=pl.CostEstimate(flops=4_000_000_000, bytes_accessed=4_000_000, transcendentals=0),
        name="layout",
    )(*arrived)


def rotated(value, axis, group, step, stride):
    count = lax.axis_size(axis)

    def target(i):
        place = i // stride % group
        return i + ((place + step) % group - place) * stride

    return lax.ppermute(value, axis, [(i, target(i)) for i in range(count)])


def local(crops, cotangent, weights):
    micro_count, channels, planes, rows, across = crops.shape
    seg = lax.axis_index("segment")
    micro, half = seg % 2, seg // 2
    devices = lax.axis_size("gy")
    swap = [(i, i ^ 1) for i in range(devices)]

    def tile(volume):
        field = lax.dynamic_index_in_dim(volume, micro, 0, keepdims=False)
        field = jnp.transpose(field, (2, 3, 1, 0)).reshape(rows, across, channels * planes)
        return lax.dynamic_slice_in_dim(field, half * 48, WIDTH, 1).reshape(rows * WIDTH, channels * planes)

    own = jnp.stack([tile(crops), tile(cotangent)])
    packed = jnp.pad(weights[0], ((0, 0), (0, 1), (0, 0), (0, 0))).reshape(2, 7, 4, channels, channels)
    packed = jnp.transpose(packed, (0, 1, 3, 2, 4)).reshape(2, 7 * channels, 4 * channels)

    others = [rotated(packed, "segment", 4, k, 1) for k in (1, 2, 3)]
    oth = lax.ppermute(own, "gy", swap)
    block = jnp.concatenate([own, oth], axis=1)

    def outward(distance):
        return [(i, (i + 2 * distance * (1 if i % 2 == 0 else -1)) % devices) for i in range(devices)]

    near = lax.ppermute(block, "gy", outward(1))
    far = lax.ppermute(block[0], "gy", outward(2))
    w1, wb = build_call(packed, *others)
    near_other = lax.ppermute(near, "gy", swap)
    far, w1 = lax.optimization_barrier((far, w1))
    far_other = lax.ppermute(far, "gy", swap)
    outs = main_call(own, oth, near, far, near_other, far_other, w1, wb)
    fields = outs[:4]
    arrived = [rotated(fields[k], "segment", 4, k, 1) for k in (1, 2, 3)]
    *keep, send = grads_call(outs[4], outs[5])

    got = lax.ppermute(send, "gy", swap)
    part = [(keep[k].astype(F32) + got[k].astype(F32)).astype(BF16) for k in range(4)]
    total = part[0].astype(F32)
    for k in (1, 2, 3):
        total = total + rotated(part[k], "segment", 4, k, 1).astype(F32)
    for stride in (2, 8):
        mine = total.astype(BF16)
        total = mine.astype(F32)
        for k in (1, 2, 3):
            total = total + rotated(mine, "gy", 4, k, stride).astype(F32)
    features, input_grads = layout_call(fields[0], *arrived)
    mine, features, input_grads = lax.optimization_barrier((total.astype(BF16), features, input_grads))
    other = lax.ppermute(mine, "gy", swap)
    low_core = lax.axis_index("gy") % 2 == 0
    both = jnp.stack([jnp.where(low_core, mine, other), jnp.where(low_core, other, mine)])
    grads = both.reshape(2, 7, channels, 4, channels).transpose(0, 1, 3, 2, 4)
    grads = grads.reshape(2, 28, channels, channels)[:, :27].astype(F32)

    shape = (1, micro_count, channels, planes, rows, across)
    return features.reshape(shape), grads[None], input_grads.reshape(shape)


def solution(mesh):
    return jax.shard_map(
        local,
        mesh=mesh,
        in_specs=(
            P(None, None, None, "gy", None),
            P(None, None, None, "gy", None),
            P("segment", None, None, None, None),
        ),
        out_specs=(
            P("segment", None, None, None, "gy", None),
            P("segment", None, None, None, None),
            P("segment", None, None, None, "gy", None),
        ),
        check_vma=False,
    )
```

```python
import jax
import jax.numpy as jnp
from jax import lax
from jax.experimental import pallas as pl
from jax.experimental.pallas import tpu as pltpu
from jax.sharding import PartitionSpec as P

ROWS = 4
WIDTH = 80
TOTAL = 36
LANES = 128
PAIRS = 4
F32 = jnp.float32
BF16 = jnp.bfloat16


def sigmoid(v):
    return 0.5 * jnp.tanh(0.5 * v) + 0.5


def slope(v):
    s = sigmoid(v)
    return s * (1.0 + v * (1.0 - s))


def at_row(row):
    return pl.multiple_of(row * WIDTH, 16)


def grouped(i):
    return lax.shift_right_logical(i, 7) * 32 + lax.bitwise_and(i, 31)


def constants():
    er = lax.broadcasted_iota(jnp.int32, (LANES, 4 * LANES), 0)
    ec = lax.broadcasted_iota(jnp.int32, (LANES, 4 * LANES), 1)
    expand = jnp.where(er == grouped(ec), 1.0, 0.0).astype(BF16)
    cr = lax.broadcasted_iota(jnp.int32, (4 * LANES, LANES), 0)
    cc = lax.broadcasted_iota(jnp.int32, (4 * LANES, LANES), 1)
    collapse = jnp.where(cc == grouped(cr), 1.0, 0.0).astype(BF16)
    plane = lax.shift_right_logical(lax.broadcasted_iota(jnp.int32, (32, LANES), 1), 5)
    return expand, collapse, [plane == z for z in range(4)]


def build_kernel(pack0, pack1, pack2, pack3, w1, wb, wpack, lx, lxt):
    seg = lax.axis_index("segment")
    for k, pack in enumerate((pack0, pack1, pack2, pack3)):
        wpack[lax.rem(seg - k + 4, 4)] = pack[...]
    expand, _, on_plane = constants()
    nothing = jnp.zeros((32, LANES), BF16)

    def place(dst, index, row, col, value):
        dst[index, row * 32 : (row + 1) * 32, col * LANES : (col + 1) * LANES] = value

    def build(index, carry):
        for dx in range(3):
            for dst in (w1, wb):
                for z in range(4):
                    place(dst, index, 12 + z, dx, nothing)
                    place(dst, index, z, 3 + dx, nothing)
        w = wpack[lax.div(index, 2), lax.rem(index, 2)]
        lx[...] = jnp.dot(w, expand, preferred_element_type=F32)
        for q in range(7):
            lxt[q * LANES : (q + 1) * LANES, :] = lax.dot_general(
                w[q * 32 : (q + 1) * 32], expand[:32, :LANES], (((0,), (0,)), ((), ())), preferred_element_type=F32
            )
        for dy in range(3):
            for dx in range(3):
                taps = [9 * dz + 3 * dy + dx for dz in range(3)]
                fwd = [lx[t // 4 * 32 : t // 4 * 32 + 32, t % 4 * LANES : (t % 4 + 1) * LANES] for t in taps]
                bwd = [lxt[t * 32 : t * 32 + 32, :] for t in taps]
                for z in range(4):
                    vf = jnp.zeros((32, LANES), F32)
                    vb = jnp.zeros((32, LANES), F32)
                    for dz in range(3):
                        if 0 <= z + 1 - dz < 4:
                            vf = jnp.where(on_plane[z + 1 - dz], fwd[dz], vf)
                        if 0 <= z + dz - 1 < 4:
                            vb = jnp.where(on_plane[z + dz - 1], bwd[dz], vb)
                    for r in range(2):
                        place(w1, index, 4 * (dy + r) + z, 3 * r + dx, vf.astype(BF16))
                        place(wb, index, 4 * (2 - dy + r) + z, 3 * r + 2 - dx, vb.astype(BF16))
        return carry

    lax.fori_loop(0, 8, build, 0)


def by_rows(v):
    return v.reshape(v.shape[0] // WIDTH, WIDTH, LANES)


def from_left(v):
    column = lax.broadcasted_iota(jnp.int32, (1, WIDTH, LANES), 1)
    return jnp.where(column == 0, 0.0, pltpu.roll(by_rows(v), 1, 1)).reshape(v.shape)


def from_right(v):
    column = lax.broadcasted_iota(jnp.int32, (1, WIDTH, LANES), 1)
    return jnp.where(column == WIDTH - 1, 0.0, pltpu.roll(by_rows(v), WIDTH - 1, 1)).reshape(v.shape)


def stacked(src, first_rows, count):
    return jnp.concatenate(
        [
            jnp.concatenate([src[(row + j) * WIDTH : (row + j + 1) * WIDTH, :] for row in first_rows], axis=0)
            for j in range(count)
        ],
        axis=1,
    )


def main_kernel(
    own, oth, near, far, near_other, far_other, w1, wb,
    out0, out1, out2, out3, windows, deltas,
    crop, cot, feats, merged, hidden, delta, sd, fd, pre1, pre2, product, out_all,
):
    seg = lax.axis_index("segment")
    gy = lax.axis_index("gy")
    core = lax.rem(gy, 2)
    half = lax.div(seg, 2)
    column = lax.broadcasted_iota(jnp.int32, (1, WIDTH, LANES), 1)

    def put(dst, row, src, src_row, rows):
        dst[row * WIDTH : (row + rows) * WIDTH, :] = src[src_row * WIDTH : (src_row + rows) * WIDTH, :]

    @pl.when(core == 0)
    def _():
        put(crop, 0, far, 0, 8)
        put(crop, 8, near.at[0], 0, 8)
        put(crop, 16, own.at[0], 0, 4)
        put(crop, 20, oth.at[0], 0, 4)
        put(crop, 24, near_other.at[0], 4, 4)
        put(crop, 28, near_other.at[0], 0, 4)
        put(crop, 32, far_other, 4, 4)
        put(cot, 0, near.at[1], 0, 8)
        put(cot, 8, own.at[1], 0, 4)
        put(cot, 12, oth.at[1], 0, 4)
        put(cot, 16, near_other.at[1], 4, 4)

    @pl.when(core == 1)
    def _():
        put(crop, 0, far_other, 4, 4)
        put(crop, 4, near_other.at[0], 0, 8)
        put(crop, 12, oth.at[0], 0, 4)
        put(crop, 16, own.at[0], 0, 4)
        put(crop, 20, near.at[0], 4, 4)
        put(crop, 24, near.at[0], 0, 4)
        put(crop, 28, far, 4, 4)
        put(crop, 32, far, 0, 4)
        put(cot, 0, near_other.at[1], 4, 4)
        put(cot, 4, oth.at[1], 0, 4)
        put(cot, 8, own.at[1], 0, 4)
        put(cot, 12, near.at[1], 4, 4)
        put(cot, 16, near.at[1], 0, 4)

    def conv(src, matrix, low, high, then):
        rows = range(low, high, 2)
        for at in range(0, len(rows), PAIRS):
            some = rows[at : at + PAIRS]
            product[at * WIDTH : (at + len(some)) * WIDTH, :] = jnp.dot(
                stacked(src, [row - 1 for row in some], 4), matrix[...], preferred_element_type=F32
            )

            def finish(i, row):
                for r in range(2):
                    block = product.at[i * WIDTH : (i + 1) * WIDTH]
                    q = [block[:, (3 * r + b) * LANES : (3 * r + b + 1) * LANES] for b in range(3)]
                    here = slice((row + r) * WIDTH, (row + r + 1) * WIDTH)
                    then(here, q[1] + from_left(q[0]) + from_right(q[2]))

            for i, row in enumerate(some):
                finish(at + i, row)

    def clear_outside(dst, low, high, first=16):
        top = first - ROWS * gy
        bottom = first + ROWS * (lax.axis_size("gy") - gy)

        def clear(i, carry):
            dst[pl.ds(at_row(i), WIDTH), :] = jnp.zeros((WIDTH, LANES), BF16)
            return carry

        @pl.when(top > low)
        def _():
            lax.fori_loop(low, jnp.minimum(top, high), clear, 0)

        @pl.when(bottom < high)
        def _():
            lax.fori_loop(jnp.maximum(bottom, low), high, clear, 0)

    clear_outside(crop, 0, 36)
    clear_outside(cot, 0, 20, 8)

    for s in range(4):
        source = crop if s == 0 else feats.at[0] if s == 1 else merged.at[s - 2]

        def first(here, v, s=s):
            pre1[s, here, :] = v
            hidden[s, here, :] = (v * sigmoid(v)).astype(BF16)

        conv(source, w1.at[2 * s], 2 * s + 1, 35 - 2 * s, first)
        clear_outside(hidden.at[s], 2 * s + 1, 35 - 2 * s)

        def second(here, v, s=s):
            pre2[s, here, :] = v
            out = (v * sigmoid(v)).astype(BF16)
            feats[s, here, :] = out
            if s == 1 or s == 2:
                skip = feats[0, here, :] if s == 1 else crop[here, :]
                merged[s - 1, here, :] = (out.astype(F32) + skip.astype(F32)).astype(BF16)

        conv(hidden.at[s], w1.at[2 * s + 1], 2 * s + 2, 34 - 2 * s, second)
        if s == 0:
            clear_outside(feats.at[0], 2, 34)
        if s == 1 or s == 2:
            clear_outside(merged.at[s - 1], 2 * s + 2, 34 - 2 * s)

    here = slice(8 * WIDTH, 28 * WIDTH)
    sd[here, :] = (cot[...].astype(F32) * slope(pre2[3, here, :])).astype(BF16)

    own_low = half * 16
    base0 = 16 * WIDTH
    slot_of = lambda s: lax.rem(s - seg + 4, 4)

    def keep(index, src, grad):
        windows[index] = src[15 * WIDTH : 21 * WIDTH, :]
        deltas[index] = grad[16 * WIDTH : 20 * WIDTH, :]

    for s in (3, 2, 1, 0):
        source = crop if s == 0 else feats.at[0] if s == 1 else merged.at[s - 2]
        low, high = 8 + 2 * (3 - s), 28 - 2 * (3 - s)

        def to_first(here, v, s=s):
            fd[here, :] = (v * slope(pre1[s, here, :])).astype(BF16)

        keep(2 * s + 1, hidden.at[s], sd)
        conv(sd, wb.at[2 * s + 1], low + 1, high - 1, to_first)
        clear_outside(fd, low + 1, high - 1)
        keep(2 * s, source, fd)

        def to_delta(here, v, s=s):
            out = v.astype(BF16)
            if s == 1 or s == 0:
                other = delta[2 if s == 1 else 3, here, :]
                out = (out.astype(F32) + other.astype(F32)).astype(BF16)
            delta[s, here, :] = out
            if s > 0:
                sd[here, :] = (
                    out.astype(F32) * slope(pre2[s - 1, here, :])
                ).astype(BF16)

        conv(fd, wb.at[2 * s], low + 2, high - 2, to_delta)
        if s > 0:
            clear_outside(sd, low + 2, high - 2)

    for s in range(4):
        for y in range(ROWS):
            place = pl.ds(pl.multiple_of(base0 + y * WIDTH + own_low, 16), 64)
            out_all[slot_of(s), 64 * y : 64 * y + 64, :] = feats[s, place, :]
            out_all[slot_of(s), 256 + 64 * y : 320 + 64 * y, :] = delta[s, place, :]
    for k, out in enumerate((out0, out1, out2, out3)):
        out[...] = out_all[k]


def grads_kernel(windows, deltas, keep0, keep1, keep2, keep3, send, grads, terms, wg_all):
    seg = lax.axis_index("segment")
    core = lax.rem(lax.axis_index("gy"), 2)
    own_low = lax.div(seg, 2) * 16
    column = lax.broadcasted_iota(jnp.int32, (1, WIDTH, LANES), 1)
    mine = (column >= own_low) & (column < own_low + 64)
    _, collapse, on_plane = constants()
    for index in range(8):
        d = jnp.where(mine, by_rows(deltas[index].astype(F32)), 0.0).reshape(ROWS * WIDTH, LANES)
        shifted = jnp.concatenate([from_right(d).astype(BF16), d.astype(BF16), from_left(d).astype(BF16)], axis=1)
        product = lax.dot_general(
            stacked(windows.at[index], range(ROWS), 3), shifted, (((0,), (0,)), ((), ())), preferred_element_type=F32
        )
        for dx in range(3):
            grads[index, dx] = product[:, dx * LANES : (dx + 1) * LANES]
        top = 224 * index
        terms[top + 6 * 32 : top + 7 * 32, 3 * LANES :] = jnp.zeros((32, LANES), BF16)
        for dy in range(3):
            for dx in range(3):
                first = [dy * LANES + z * 32 for z in range(4)]
                rows = [grads[index, dx, at : at + 32, :] for at in first]
                for dz in range(3):
                    total = jnp.zeros((32, LANES), F32)
                    for z in range(4):
                        if 0 <= z + 1 - dz < 4:
                            total = jnp.where(on_plane[z + 1 - dz], rows[z], total)
                    t = 9 * dz + 3 * dy + dx
                    at = top + t // 4 * 32
                    terms[at : at + 32, t % 4 * LANES : (t % 4 + 1) * LANES] = total.astype(BF16)
    packed = jnp.dot(terms[...], collapse, preferred_element_type=F32).astype(BF16)
    for s in range(4):
        for which in range(2):
            top = 224 * (2 * s + which)
            wg_all[which, lax.rem(s - seg + 4, 4)] = packed[top : top + 224]
    for k, keep in enumerate((keep0, keep1, keep2, keep3)):
        keep[...] = wg_all[core, k]
    send[...] = wg_all[1 - core]


VMEM = pl.BlockSpec(memory_space=pltpu.VMEM)
MATRICES = (8, 4 * LANES, 6 * LANES)


def build_call(*packs):
    return pl.pallas_call(
        build_kernel,
        out_shape=[jax.ShapeDtypeStruct(MATRICES, BF16)] * 2,
        in_specs=[VMEM] * 4,
        out_specs=[VMEM] * 2,
        scratch_shapes=[
            pltpu.VMEM((4, 2, 224, LANES), BF16),
            pltpu.VMEM((224, 4 * LANES), F32),
            pltpu.VMEM((7 * LANES, LANES), F32),
        ],
        compiler_params=pltpu.CompilerParams(vmem_limit_bytes=8 * 1024 * 1024),
        cost_estimate=pl.CostEstimate(flops=5_000_000_000, bytes_accessed=10_000_000, transcendentals=0),
        name="banded",
    )(*packs)


def main_call(*operands):
    acts = (TOTAL * WIDTH, LANES)
    return pl.pallas_call(
        main_kernel,
        out_shape=[jax.ShapeDtypeStruct((512, LANES), BF16)] * 4
        + [
            jax.ShapeDtypeStruct((8, 6 * WIDTH, LANES), BF16),
            jax.ShapeDtypeStruct((8, 4 * WIDTH, LANES), BF16),
        ],
        in_specs=[VMEM] * 8,
        out_specs=[VMEM] * 6,
        scratch_shapes=[
            pltpu.VMEM(acts, BF16),
            pltpu.VMEM((20 * WIDTH, LANES), BF16),
            pltpu.VMEM((4,) + acts, BF16),
            pltpu.VMEM((2,) + acts, BF16),
            pltpu.VMEM((4,) + acts, BF16),
            pltpu.VMEM((4,) + acts, BF16),
            pltpu.VMEM(acts, BF16),
            pltpu.VMEM(acts, BF16),
            pltpu.VMEM((4,) + acts, F32),
            pltpu.VMEM((4,) + acts, F32),
            pltpu.VMEM((17 * WIDTH, 6 * LANES), F32),
            pltpu.VMEM((4, 512, LANES), BF16),
        ],
        compiler_params=pltpu.CompilerParams(vmem_limit_bytes=36 * 1024 * 1024),
        cost_estimate=pl.CostEstimate(flops=20_000_000_000, bytes_accessed=10_000_000, transcendentals=0),
        name="sections",
    )(*operands)


def grads_call(windows, deltas):
    return pl.pallas_call(
        grads_kernel,
        out_shape=[jax.ShapeDtypeStruct((224, LANES), BF16)] * 4 + [jax.ShapeDtypeStruct((4, 224, LANES), BF16)],
        in_specs=[VMEM] * 2,
        out_specs=[VMEM] * 5,
        scratch_shapes=[
            pltpu.VMEM((8, 3, 3 * LANES, LANES), F32),
            pltpu.VMEM((8 * 224, 4 * LANES), BF16),
            pltpu.VMEM((2, 4, 224, LANES), BF16),
        ],
        compiler_params=pltpu.CompilerParams(vmem_limit_bytes=16 * 1024 * 1024),
        cost_estimate=pl.CostEstimate(flops=6_000_000_000, bytes_accessed=4_000_000, transcendentals=0),
        name="kernel_grads",
    )(windows, deltas)


def layout_kernel(in0, in1, in2, in3, features, gradients, by_source):
    seg = lax.axis_index("segment")
    for k, arrived in enumerate((in0, in1, in2, in3)):
        by_source[lax.rem(seg - k + 4, 4)] = arrived[...]
    for which, out in enumerate((features, gradients)):
        for m in range(2):
            planes = []
            for y in range(ROWS):
                start = 256 * which + 64 * y
                row = jnp.concatenate([by_source[m, start : start + 64, :], by_source[2 + m, start : start + 64, :]])
                planes.append(row.astype(F32).T[:, None, :])
            for z in range(4):
                part = [plane[32 * z : 32 * z + 32] for plane in planes]
                out[m, :, z] = jnp.concatenate(part, axis=1).astype(out.dtype)


def layout_call(*arrived):
    return pl.pallas_call(
        layout_kernel,
        out_shape=[
            jax.ShapeDtypeStruct((2, 32, 4, ROWS, LANES), BF16),
            jax.ShapeDtypeStruct((2, 32, 4, ROWS, LANES), F32),
        ],
        in_specs=[VMEM] * 4,
        out_specs=[VMEM] * 2,
        scratch_shapes=[pltpu.VMEM((4, 512, LANES), BF16)],
        compiler_params=pltpu.CompilerParams(vmem_limit_bytes=8 * 1024 * 1024),
        cost_estimate=pl.CostEstimate(flops=4_000_000_000, bytes_accessed=4_000_000, transcendentals=0),
        name="layout",
    )(*arrived)


def rotated(value, axis, group, step, stride):
    count = lax.axis_size(axis)

    def target(i):
        place = i // stride % group
        return i + ((place + step) % group - place) * stride

    return lax.ppermute(value, axis, [(i, target(i)) for i in range(count)])


def local(crops, cotangent, weights):
    micro_count, channels, planes, rows, across = crops.shape
    seg = lax.axis_index("segment")
    micro, half = seg % 2, seg // 2
    devices = lax.axis_size("gy")
    swap = [(i, i ^ 1) for i in range(devices)]

    def tile(volume):
        field = lax.dynamic_index_in_dim(volume, micro, 0, keepdims=False)
        field = jnp.transpose(field, (2, 3, 1, 0)).reshape(rows, across, channels * planes)
        return lax.dynamic_slice_in_dim(field, half * 48, WIDTH, 1).reshape(rows * WIDTH, channels * planes)

    own = jnp.stack([tile(crops), tile(cotangent)])
    packed = jnp.pad(weights[0], ((0, 0), (0, 1), (0, 0), (0, 0))).reshape(2, 7, 4, channels, channels)
    packed = jnp.transpose(packed, (0, 1, 3, 2, 4)).reshape(2, 7 * channels, 4 * channels)

    others = [rotated(packed, "segment", 4, k, 1) for k in (1, 2, 3)]
    oth = lax.ppermute(own, "gy", swap)
    oth, packed = lax.optimization_barrier((oth, packed))
    block = jnp.concatenate([own, oth], axis=1)

    def outward(distance):
        return [(i, (i + 2 * distance * (1 if i % 2 == 0 else -1)) % devices) for i in range(devices)]

    near = lax.ppermute(block, "gy", outward(1))
    far = lax.ppermute(block[0], "gy", outward(2))
    w1, wb = build_call(packed, *others)
    near_other = lax.ppermute(near, "gy", swap)
    far, w1 = lax.optimization_barrier((far, w1))
    far_other = lax.ppermute(far, "gy", swap)
    outs = main_call(own, oth, near, far, near_other, far_other, w1, wb)
    fields = outs[:4]
    arrived = [rotated(fields[k], "segment", 4, k, 1) for k in (1, 2, 3)]
    *keep, send = grads_call(outs[4], outs[5])

    got = lax.ppermute(send, "gy", swap)
    part = [(keep[k].astype(F32) + got[k].astype(F32)).astype(BF16) for k in range(4)]
    total = part[0].astype(F32)
    for k in (1, 2, 3):
        total = total + rotated(part[k], "segment", 4, k, 1).astype(F32)
    for stride in (2, 8):
        mine = total.astype(BF16)
        total = mine.astype(F32)
        for k in (1, 2, 3):
            total = total + rotated(mine, "gy", 4, k, stride).astype(F32)
    features, input_grads = layout_call(fields[0], *arrived)
    mine, features, input_grads = lax.optimization_barrier((total.astype(BF16), features, input_grads))
    other = lax.ppermute(mine, "gy", swap)
    low_core = lax.axis_index("gy") % 2 == 0
    both = jnp.stack([jnp.where(low_core, mine, other), jnp.where(low_core, other, mine)])
    grads = both.reshape(2, 7, channels, 4, channels).transpose(0, 1, 3, 2, 4)
    grads = grads.reshape(2, 28, channels, channels)[:, :27].astype(F32)

    shape = (1, micro_count, channels, planes, rows, across)
    return features.reshape(shape), grads[None], input_grads.reshape(shape)


def solution(mesh):
    return jax.shard_map(
        local,
        mesh=mesh,
        in_specs=(
            P(None, None, None, "gy", None),
            P(None, None, None, "gy", None),
            P("segment", None, None, None, None),
        ),
        out_specs=(
            P("segment", None, None, None, "gy", None),
            P("segment", None, None, None, None),
            P("segment", None, None, None, "gy", None),
        ),
        check_vma=False,
    )
```

```python
import jax
import jax.numpy as jnp
from jax import lax
from jax.experimental import pallas as pl
from jax.experimental.pallas import tpu as pltpu
from jax.sharding import PartitionSpec as P

ROWS = 4
WIDTH = 80
TOTAL = 36
LANES = 128
PAIRS = 4
F32 = jnp.float32
BF16 = jnp.bfloat16


def sigmoid(v):
    return 0.5 * jnp.tanh(0.5 * v) + 0.5


def slope(v):
    s = sigmoid(v)
    return s * (1.0 + v * (1.0 - s))


def at_row(row):
    return pl.multiple_of(row * WIDTH, 16)


def grouped(i):
    return lax.shift_right_logical(i, 7) * 32 + lax.bitwise_and(i, 31)


def constants():
    er = lax.broadcasted_iota(jnp.int32, (LANES, 4 * LANES), 0)
    ec = lax.broadcasted_iota(jnp.int32, (LANES, 4 * LANES), 1)
    expand = jnp.where(er == grouped(ec), 1.0, 0.0).astype(BF16)
    cr = lax.broadcasted_iota(jnp.int32, (4 * LANES, LANES), 0)
    cc = lax.broadcasted_iota(jnp.int32, (4 * LANES, LANES), 1)
    collapse = jnp.where(cc == grouped(cr), 1.0, 0.0).astype(BF16)
    plane = lax.shift_right_logical(lax.broadcasted_iota(jnp.int32, (32, LANES), 1), 5)
    return expand, collapse, [plane == z for z in range(4)]


def build_kernel(pack0, half1, half2, half3, rest1, rest2, rest3, w1, wb, wpack, lx, lxt):
    seg = lax.axis_index("segment")
    core = lax.rem(lax.axis_index("gy"), 2)
    wpack[seg] = pack0[...]
    for k, half, rest in ((1, half1, rest1), (2, half2, rest2), (3, half3, rest3)):
        wpack[lax.rem(seg - k + 4, 4), core] = half[...]
        wpack[lax.rem(seg - k + 4, 4), 1 - core] = rest[...]
    expand, _, on_plane = constants()
    nothing = jnp.zeros((32, LANES), BF16)

    def place(dst, index, row, col, value):
        dst[index, row * 32 : (row + 1) * 32, col * LANES : (col + 1) * LANES] = value

    def build(index, carry):
        for dx in range(3):
            for dst in (w1, wb):
                for z in range(4):
                    place(dst, index, 12 + z, dx, nothing)
                    place(dst, index, z, 3 + dx, nothing)
        w = wpack[lax.div(index, 2), lax.rem(index, 2)]
        lx[...] = jnp.dot(w, expand, preferred_element_type=F32)
        for q in range(7):
            lxt[q * LANES : (q + 1) * LANES, :] = lax.dot_general(
                w[q * 32 : (q + 1) * 32], expand[:32, :LANES], (((0,), (0,)), ((), ())), preferred_element_type=F32
            )
        for dy in range(3):
            for dx in range(3):
                taps = [9 * dz + 3 * dy + dx for dz in range(3)]
                fwd = [lx[t // 4 * 32 : t // 4 * 32 + 32, t % 4 * LANES : (t % 4 + 1) * LANES] for t in taps]
                bwd = [lxt[t * 32 : t * 32 + 32, :] for t in taps]
                for z in range(4):
                    vf = jnp.zeros((32, LANES), F32)
                    vb = jnp.zeros((32, LANES), F32)
                    for dz in range(3):
                        if 0 <= z + 1 - dz < 4:
                            vf = jnp.where(on_plane[z + 1 - dz], fwd[dz], vf)
                        if 0 <= z + dz - 1 < 4:
                            vb = jnp.where(on_plane[z + dz - 1], bwd[dz], vb)
                    for r in range(2):
                        place(w1, index, 4 * (dy + r) + z, 3 * r + dx, vf.astype(BF16))
                        place(wb, index, 4 * (2 - dy + r) + z, 3 * r + 2 - dx, vb.astype(BF16))
        return carry

    lax.fori_loop(0, 8, build, 0)


def by_rows(v):
    return v.reshape(v.shape[0] // WIDTH, WIDTH, LANES)


def from_left(v):
    column = lax.broadcasted_iota(jnp.int32, (1, WIDTH, LANES), 1)
    return jnp.where(column == 0, 0.0, pltpu.roll(by_rows(v), 1, 1)).reshape(v.shape)


def from_right(v):
    column = lax.broadcasted_iota(jnp.int32, (1, WIDTH, LANES), 1)
    return jnp.where(column == WIDTH - 1, 0.0, pltpu.roll(by_rows(v), WIDTH - 1, 1)).reshape(v.shape)


def stacked(src, first_rows, count):
    return jnp.concatenate(
        [
            jnp.concatenate([src[(row + j) * WIDTH : (row + j + 1) * WIDTH, :] for row in first_rows], axis=0)
            for j in range(count)
        ],
        axis=1,
    )


def main_kernel(
    own, oth, near, far, near_other, far_other, w1, wb,
    out0, out1, out2, out3, windows, deltas,
    crop, cot, feats, merged, hidden, delta, sd, fd, pre1, pre2, product, out_all,
):
    seg = lax.axis_index("segment")
    gy = lax.axis_index("gy")
    core = lax.rem(gy, 2)
    half = lax.div(seg, 2)
    column = lax.broadcasted_iota(jnp.int32, (1, WIDTH, LANES), 1)

    def put(dst, row, src, src_row, rows):
        dst[row * WIDTH : (row + rows) * WIDTH, :] = src[src_row * WIDTH : (src_row + rows) * WIDTH, :]

    @pl.when(core == 0)
    def _():
        put(crop, 0, far, 0, 8)
        put(crop, 8, near.at[0], 0, 8)
        put(crop, 16, own.at[0], 0, 4)
        put(crop, 20, oth.at[0], 0, 4)
        put(crop, 24, near_other.at[0], 4, 4)
        put(crop, 28, near_other.at[0], 0, 4)
        put(crop, 32, far_other, 4, 4)
        put(cot, 0, near.at[1], 0, 8)
        put(cot, 8, own.at[1], 0, 4)
        put(cot, 12, oth.at[1], 0, 4)
        put(cot, 16, near_other.at[1], 4, 4)

    @pl.when(core == 1)
    def _():
        put(crop, 0, far_other, 4, 4)
        put(crop, 4, near_other.at[0], 0, 8)
        put(crop, 12, oth.at[0], 0, 4)
        put(crop, 16, own.at[0], 0, 4)
        put(crop, 20, near.at[0], 4, 4)
        put(crop, 24, near.at[0], 0, 4)
        put(crop, 28, far, 4, 4)
        put(crop, 32, far, 0, 4)
        put(cot, 0, near_other.at[1], 4, 4)
        put(cot, 4, oth.at[1], 0, 4)
        put(cot, 8, own.at[1], 0, 4)
        put(cot, 12, near.at[1], 4, 4)
        put(cot, 16, near.at[1], 0, 4)

    def conv(src, matrix, low, high, then):
        rows = range(low, high, 2)
        for at in range(0, len(rows), PAIRS):
            some = rows[at : at + PAIRS]
            product[at * WIDTH : (at + len(some)) * WIDTH, :] = jnp.dot(
                stacked(src, [row - 1 for row in some], 4), matrix[...], preferred_element_type=F32
            )

            def finish(i, row):
                for r in range(2):
                    block = product.at[i * WIDTH : (i + 1) * WIDTH]
                    q = [block[:, (3 * r + b) * LANES : (3 * r + b + 1) * LANES] for b in range(3)]
                    here = slice((row + r) * WIDTH, (row + r + 1) * WIDTH)
                    then(here, q[1] + from_left(q[0]) + from_right(q[2]))

            for i, row in enumerate(some):
                finish(at + i, row)

    def clear_outside(dst, low, high, first=16):
        top = first - ROWS * gy
        bottom = first + ROWS * (lax.axis_size("gy") - gy)

        def clear(i, carry):
            dst[pl.ds(at_row(i), WIDTH), :] = jnp.zeros((WIDTH, LANES), BF16)
            return carry

        @pl.when(top > low)
        def _():
            lax.fori_loop(low, jnp.minimum(top, high), clear, 0)

        @pl.when(bottom < high)
        def _():
            lax.fori_loop(jnp.maximum(bottom, low), high, clear, 0)

    clear_outside(crop, 0, 36)
    clear_outside(cot, 0, 20, 8)

    for s in range(4):
        source = crop if s == 0 else feats.at[0] if s == 1 else merged.at[s - 2]

        def first(here, v, s=s):
            pre1[s, here, :] = v
            hidden[s, here, :] = (v * sigmoid(v)).astype(BF16)

        conv(source, w1.at[2 * s], 2 * s + 1, 35 - 2 * s, first)
        clear_outside(hidden.at[s], 2 * s + 1, 35 - 2 * s)

        def second(here, v, s=s):
            pre2[s, here, :] = v
            out = (v * sigmoid(v)).astype(BF16)
            feats[s, here, :] = out
            if s == 1 or s == 2:
                skip = feats[0, here, :] if s == 1 else crop[here, :]
                merged[s - 1, here, :] = (out.astype(F32) + skip.astype(F32)).astype(BF16)

        conv(hidden.at[s], w1.at[2 * s + 1], 2 * s + 2, 34 - 2 * s, second)
        if s == 0:
            clear_outside(feats.at[0], 2, 34)
        if s == 1 or s == 2:
            clear_outside(merged.at[s - 1], 2 * s + 2, 34 - 2 * s)

    here = slice(8 * WIDTH, 28 * WIDTH)
    sd[here, :] = (cot[...].astype(F32) * slope(pre2[3, here, :])).astype(BF16)

    own_low = half * 16
    base0 = 16 * WIDTH
    slot_of = lambda s: lax.rem(s - seg + 4, 4)

    def keep(index, src, grad):
        windows[index] = src[15 * WIDTH : 21 * WIDTH, :]
        deltas[index] = grad[16 * WIDTH : 20 * WIDTH, :]

    for s in (3, 2, 1, 0):
        source = crop if s == 0 else feats.at[0] if s == 1 else merged.at[s - 2]
        low, high = 8 + 2 * (3 - s), 28 - 2 * (3 - s)

        def to_first(here, v, s=s):
            fd[here, :] = (v * slope(pre1[s, here, :])).astype(BF16)

        keep(2 * s + 1, hidden.at[s], sd)
        conv(sd, wb.at[2 * s + 1], low + 1, high - 1, to_first)
        clear_outside(fd, low + 1, high - 1)
        keep(2 * s, source, fd)

        def to_delta(here, v, s=s):
            out = v.astype(BF16)
            if s == 1 or s == 0:
                other = delta[2 if s == 1 else 3, here, :]
                out = (out.astype(F32) + other.astype(F32)).astype(BF16)
            delta[s, here, :] = out
            if s > 0:
                sd[here, :] = (
                    out.astype(F32) * slope(pre2[s - 1, here, :])
                ).astype(BF16)

        conv(fd, wb.at[2 * s], low + 2, high - 2, to_delta)
        if s > 0:
            clear_outside(sd, low + 2, high - 2)

    for s in range(4):
        for y in range(ROWS):
            place = pl.ds(pl.multiple_of(base0 + y * WIDTH + own_low, 16), 64)
            out_all[slot_of(s), 64 * y : 64 * y + 64, :] = feats[s, place, :]
            out_all[slot_of(s), 256 + 64 * y : 320 + 64 * y, :] = delta[s, place, :]
    for k, out in enumerate((out0, out1, out2, out3)):
        out[...] = out_all[k]


def grads_kernel(windows, deltas, keep0, keep1, keep2, keep3, send, grads, terms, wg_all):
    seg = lax.axis_index("segment")
    core = lax.rem(lax.axis_index("gy"), 2)
    own_low = lax.div(seg, 2) * 16
    column = lax.broadcasted_iota(jnp.int32, (1, WIDTH, LANES), 1)
    mine = (column >= own_low) & (column < own_low + 64)
    _, collapse, on_plane = constants()
    for index in range(8):
        d = jnp.where(mine, by_rows(deltas[index].astype(F32)), 0.0).reshape(ROWS * WIDTH, LANES)
        shifted = jnp.concatenate([from_right(d).astype(BF16), d.astype(BF16), from_left(d).astype(BF16)], axis=1)
        product = lax.dot_general(
            stacked(windows.at[index], range(ROWS), 3), shifted, (((0,), (0,)), ((), ())), preferred_element_type=F32
        )
        for dx in range(3):
            grads[index, dx] = product[:, dx * LANES : (dx + 1) * LANES]
        top = 224 * index
        terms[top + 6 * 32 : top + 7 * 32, 3 * LANES :] = jnp.zeros((32, LANES), BF16)
        for dy in range(3):
            for dx in range(3):
                first = [dy * LANES + z * 32 for z in range(4)]
                rows = [grads[index, dx, at : at + 32, :] for at in first]
                for dz in range(3):
                    total = jnp.zeros((32, LANES), F32)
                    for z in range(4):
                        if 0 <= z + 1 - dz < 4:
                            total = jnp.where(on_plane[z + 1 - dz], rows[z], total)
                    t = 9 * dz + 3 * dy + dx
                    at = top + t // 4 * 32
                    terms[at : at + 32, t % 4 * LANES : (t % 4 + 1) * LANES] = total.astype(BF16)
    packed = jnp.dot(terms[...], collapse, preferred_element_type=F32).astype(BF16)
    for s in range(4):
        for which in range(2):
            top = 224 * (2 * s + which)
            wg_all[which, lax.rem(s - seg + 4, 4)] = packed[top : top + 224]
    for k, keep in enumerate((keep0, keep1, keep2, keep3)):
        keep[...] = wg_all[core, k]
    send[...] = wg_all[1 - core]


VMEM = pl.BlockSpec(memory_space=pltpu.VMEM)
MATRICES = (8, 4 * LANES, 6 * LANES)


def build_call(*packs):
    return pl.pallas_call(
        build_kernel,
        out_shape=[jax.ShapeDtypeStruct(MATRICES, BF16)] * 2,
        in_specs=[VMEM] * 7,
        out_specs=[VMEM] * 2,
        scratch_shapes=[
            pltpu.VMEM((4, 2, 224, LANES), BF16),
            pltpu.VMEM((224, 4 * LANES), F32),
            pltpu.VMEM((7 * LANES, LANES), F32),
        ],
        compiler_params=pltpu.CompilerParams(vmem_limit_bytes=8 * 1024 * 1024),
        cost_estimate=pl.CostEstimate(flops=5_000_000_000, bytes_accessed=10_000_000, transcendentals=0),
        name="banded",
    )(*packs)


def main_call(*operands):
    acts = (TOTAL * WIDTH, LANES)
    return pl.pallas_call(
        main_kernel,
        out_shape=[jax.ShapeDtypeStruct((512, LANES), BF16)] * 4
        + [
            jax.ShapeDtypeStruct((8, 6 * WIDTH, LANES), BF16),
            jax.ShapeDtypeStruct((8, 4 * WIDTH, LANES), BF16),
        ],
        in_specs=[VMEM] * 8,
        out_specs=[VMEM] * 6,
        scratch_shapes=[
            pltpu.VMEM(acts, BF16),
            pltpu.VMEM((20 * WIDTH, LANES), BF16),
            pltpu.VMEM((4,) + acts, BF16),
            pltpu.VMEM((2,) + acts, BF16),
            pltpu.VMEM((4,) + acts, BF16),
            pltpu.VMEM((4,) + acts, BF16),
            pltpu.VMEM(acts, BF16),
            pltpu.VMEM(acts, BF16),
            pltpu.VMEM((4,) + acts, F32),
            pltpu.VMEM((4,) + acts, F32),
            pltpu.VMEM((17 * WIDTH, 6 * LANES), F32),
            pltpu.VMEM((4, 512, LANES), BF16),
        ],
        compiler_params=pltpu.CompilerParams(vmem_limit_bytes=36 * 1024 * 1024),
        cost_estimate=pl.CostEstimate(flops=20_000_000_000, bytes_accessed=10_000_000, transcendentals=0),
        name="sections",
    )(*operands)


def grads_call(windows, deltas):
    return pl.pallas_call(
        grads_kernel,
        out_shape=[jax.ShapeDtypeStruct((224, LANES), BF16)] * 4 + [jax.ShapeDtypeStruct((4, 224, LANES), BF16)],
        in_specs=[VMEM] * 2,
        out_specs=[VMEM] * 5,
        scratch_shapes=[
            pltpu.VMEM((8, 3, 3 * LANES, LANES), F32),
            pltpu.VMEM((8 * 224, 4 * LANES), BF16),
            pltpu.VMEM((2, 4, 224, LANES), BF16),
        ],
        compiler_params=pltpu.CompilerParams(vmem_limit_bytes=16 * 1024 * 1024),
        cost_estimate=pl.CostEstimate(flops=6_000_000_000, bytes_accessed=4_000_000, transcendentals=0),
        name="kernel_grads",
    )(windows, deltas)


def layout_kernel(in0, in1, in2, in3, features, gradients, by_source):
    seg = lax.axis_index("segment")
    for k, arrived in enumerate((in0, in1, in2, in3)):
        by_source[lax.rem(seg - k + 4, 4)] = arrived[...]
    for which, out in enumerate((features, gradients)):
        for m in range(2):
            planes = []
            for y in range(ROWS):
                start = 256 * which + 64 * y
                row = jnp.concatenate([by_source[m, start : start + 64, :], by_source[2 + m, start : start + 64, :]])
                planes.append(row.astype(F32).T[:, None, :])
            for z in range(4):
                part = [plane[32 * z : 32 * z + 32] for plane in planes]
                out[m, :, z] = jnp.concatenate(part, axis=1).astype(out.dtype)


def layout_call(*arrived):
    return pl.pallas_call(
        layout_kernel,
        out_shape=[
            jax.ShapeDtypeStruct((2, 32, 4, ROWS, LANES), BF16),
            jax.ShapeDtypeStruct((2, 32, 4, ROWS, LANES), F32),
        ],
        in_specs=[VMEM] * 4,
        out_specs=[VMEM] * 2,
        scratch_shapes=[pltpu.VMEM((4, 512, LANES), BF16)],
        compiler_params=pltpu.CompilerParams(vmem_limit_bytes=8 * 1024 * 1024),
        cost_estimate=pl.CostEstimate(flops=4_000_000_000, bytes_accessed=4_000_000, transcendentals=0),
        name="layout",
    )(*arrived)


def rotated(value, axis, group, step, stride):
    count = lax.axis_size(axis)

    def target(i):
        place = i // stride % group
        return i + ((place + step) % group - place) * stride

    return lax.ppermute(value, axis, [(i, target(i)) for i in range(count)])


def local(crops, cotangent, weights):
    micro_count, channels, planes, rows, across = crops.shape
    seg = lax.axis_index("segment")
    micro, half = seg % 2, seg // 2
    devices = lax.axis_size("gy")
    swap = [(i, i ^ 1) for i in range(devices)]

    def tile(volume):
        field = lax.dynamic_index_in_dim(volume, micro, 0, keepdims=False)
        field = jnp.transpose(field, (2, 3, 1, 0)).reshape(rows, across, channels * planes)
        return lax.dynamic_slice_in_dim(field, half * 48, WIDTH, 1).reshape(rows * WIDTH, channels * planes)

    own = jnp.stack([tile(crops), tile(cotangent)])
    packed = jnp.pad(weights[0], ((0, 0), (0, 1), (0, 0), (0, 0))).reshape(2, 7, 4, channels, channels)
    packed = jnp.transpose(packed, (0, 1, 3, 2, 4)).reshape(2, 7 * channels, 4 * channels)

    share = lax.dynamic_index_in_dim(packed, lax.axis_index("gy") % 2, 0, keepdims=False)
    others = [rotated(share, "segment", 4, k, 1) for k in (1, 2, 3)]
    others += [lax.ppermute(other, "gy", swap) for other in others]
    oth = lax.ppermute(own, "gy", swap)
    oth, packed = lax.optimization_barrier((oth, packed))
    block = jnp.concatenate([own, oth], axis=1)

    def outward(distance):
        return [(i, (i + 2 * distance * (1 if i % 2 == 0 else -1)) % devices) for i in range(devices)]

    near = lax.ppermute(block, "gy", outward(1))
    far = lax.ppermute(block[0], "gy", outward(2))
    w1, wb = build_call(packed, *others)
    near_other = lax.ppermute(near, "gy", swap)
    far_other = lax.ppermute(far, "gy", swap)
    outs = main_call(own, oth, near, far, near_other, far_other, w1, wb)
    fields = outs[:4]
    arrived = [rotated(fields[k], "segment", 4, k, 1) for k in (1, 2, 3)]
    *keep, send = grads_call(outs[4], outs[5])

    got = lax.ppermute(send, "gy", swap)
    part = [(keep[k].astype(F32) + got[k].astype(F32)).astype(BF16) for k in range(4)]
    total = part[0].astype(F32)
    for k in (1, 2, 3):
        total = total + rotated(part[k], "segment", 4, k, 1).astype(F32)
    for stride in (2, 8):
        mine = total.astype(BF16)
        total = mine.astype(F32)
        for k in (1, 2, 3):
            total = total + rotated(mine, "gy", 4, k, stride).astype(F32)
    features, input_grads = layout_call(fields[0], *arrived)
    mine, features, input_grads = lax.optimization_barrier((total.astype(BF16), features, input_grads))
    other = lax.ppermute(mine, "gy", swap)
    low_core = lax.axis_index("gy") % 2 == 0
    both = jnp.stack([jnp.where(low_core, mine, other), jnp.where(low_core, other, mine)])
    grads = both.reshape(2, 7, channels, 4, channels).transpose(0, 1, 3, 2, 4)
    grads = grads.reshape(2, 28, channels, channels)[:, :27].astype(F32)

    shape = (1, micro_count, channels, planes, rows, across)
    return features.reshape(shape), grads[None], input_grads.reshape(shape)


def solution(mesh):
    return jax.shard_map(
        local,
        mesh=mesh,
        in_specs=(
            P(None, None, None, "gy", None),
            P(None, None, None, "gy", None),
            P("segment", None, None, None, None),
        ),
        out_specs=(
            P("segment", None, None, None, "gy", None),
            P("segment", None, None, None, None),
            P("segment", None, None, None, "gy", None),
        ),
        check_vma=False,
    )
```

```python
import jax
import jax.numpy as jnp
from jax import lax
from jax.experimental import pallas as pl
from jax.experimental.pallas import tpu as pltpu
from jax.sharding import PartitionSpec as P

ROWS = 4
WIDTH = 80
TOTAL = 36
LANES = 128
PAIRS = 4
F32 = jnp.float32
BF16 = jnp.bfloat16


def sigmoid(v):
    return 0.5 * jnp.tanh(0.5 * v) + 0.5


def slope(v):
    s = sigmoid(v)
    return s * (1.0 + v * (1.0 - s))


def at_row(row):
    return pl.multiple_of(row * WIDTH, 16)


def grouped(i):
    return lax.shift_right_logical(i, 7) * 32 + lax.bitwise_and(i, 31)


def constants():
    er = lax.broadcasted_iota(jnp.int32, (LANES, 4 * LANES), 0)
    ec = lax.broadcasted_iota(jnp.int32, (LANES, 4 * LANES), 1)
    expand = jnp.where(er == grouped(ec), 1.0, 0.0).astype(BF16)
    cr = lax.broadcasted_iota(jnp.int32, (4 * LANES, LANES), 0)
    cc = lax.broadcasted_iota(jnp.int32, (4 * LANES, LANES), 1)
    collapse = jnp.where(cc == grouped(cr), 1.0, 0.0).astype(BF16)
    plane = lax.shift_right_logical(lax.broadcasted_iota(jnp.int32, (32, LANES), 1), 5)
    return expand, collapse, [plane == z for z in range(4)]


def build_kernel(pack0, half1, half2, half3, rest1, rest2, rest3, w1, wb, wpack, lx, lxt):
    seg = lax.axis_index("segment")
    core = lax.rem(lax.axis_index("gy"), 2)
    wpack[seg] = pack0[...]
    for k, half, rest in ((1, half1, rest1), (2, half2, rest2), (3, half3, rest3)):
        wpack[lax.rem(seg - k + 4, 4), core] = half[...]
        wpack[lax.rem(seg - k + 4, 4), 1 - core] = rest[...]
    expand, _, on_plane = constants()
    nothing = jnp.zeros((32, LANES), BF16)

    def place(dst, index, row, col, value):
        dst[index, row * 32 : (row + 1) * 32, col * LANES : (col + 1) * LANES] = value

    def build(index, carry):
        for dx in range(3):
            for dst in (w1, wb):
                for z in range(4):
                    place(dst, index, 12 + z, dx, nothing)
                    place(dst, index, z, 3 + dx, nothing)
        w = wpack[lax.div(index, 2), lax.rem(index, 2)]
        lx[...] = jnp.dot(w, expand, preferred_element_type=F32)
        for q in range(7):
            lxt[q * LANES : (q + 1) * LANES, :] = lax.dot_general(
                w[q * 32 : (q + 1) * 32], expand[:32, :LANES], (((0,), (0,)), ((), ())), preferred_element_type=F32
            )
        for dy in range(3):
            for dx in range(3):
                taps = [9 * dz + 3 * dy + dx for dz in range(3)]
                fwd = [lx[t // 4 * 32 : t // 4 * 32 + 32, t % 4 * LANES : (t % 4 + 1) * LANES] for t in taps]
                bwd = [lxt[t * 32 : t * 32 + 32, :] for t in taps]
                for z in range(4):
                    vf = jnp.zeros((32, LANES), F32)
                    vb = jnp.zeros((32, LANES), F32)
                    for dz in range(3):
                        if 0 <= z + 1 - dz < 4:
                            vf = jnp.where(on_plane[z + 1 - dz], fwd[dz], vf)
                        if 0 <= z + dz - 1 < 4:
                            vb = jnp.where(on_plane[z + dz - 1], bwd[dz], vb)
                    for r in range(2):
                        place(w1, index, 4 * (dy + r) + z, 3 * r + dx, vf.astype(BF16))
                        place(wb, index, 4 * (2 - dy + r) + z, 3 * r + 2 - dx, vb.astype(BF16))
        return carry

    lax.fori_loop(0, 8, build, 0)


def by_rows(v):
    return v.reshape(v.shape[0] // WIDTH, WIDTH, LANES)


def from_left(v):
    column = lax.broadcasted_iota(jnp.int32, (1, WIDTH, LANES), 1)
    return jnp.where(column == 0, 0.0, pltpu.roll(by_rows(v), 1, 1)).reshape(v.shape)


def from_right(v):
    column = lax.broadcasted_iota(jnp.int32, (1, WIDTH, LANES), 1)
    return jnp.where(column == WIDTH - 1, 0.0, pltpu.roll(by_rows(v), WIDTH - 1, 1)).reshape(v.shape)


def stacked(src, first_rows, count):
    return jnp.concatenate(
        [
            jnp.concatenate([src[(row + j) * WIDTH : (row + j + 1) * WIDTH, :] for row in first_rows], axis=0)
            for j in range(count)
        ],
        axis=1,
    )


def main_kernel(
    own, oth, near, far, near_other, far_other, w1, wb,
    out0, out1, out2, out3, windows, deltas,
    crop, cot, feats, merged, hidden, delta, sd, fd, pre1, pre2, product, out_all,
):
    seg = lax.axis_index("segment")
    gy = lax.axis_index("gy")
    core = lax.rem(gy, 2)
    half = lax.div(seg, 2)
    column = lax.broadcasted_iota(jnp.int32, (1, WIDTH, LANES), 1)

    def put(dst, row, src, src_row, rows):
        dst[row * WIDTH : (row + rows) * WIDTH, :] = src[src_row * WIDTH : (src_row + rows) * WIDTH, :]

    @pl.when(core == 0)
    def _():
        put(crop, 0, far, 0, 8)
        put(crop, 8, near.at[0], 0, 8)
        put(crop, 16, own.at[0], 0, 4)
        put(crop, 20, oth.at[0], 0, 4)
        put(crop, 24, near_other.at[0], 4, 4)
        put(crop, 28, near_other.at[0], 0, 4)
        put(crop, 32, far_other, 4, 4)
        put(cot, 0, near.at[1], 0, 8)
        put(cot, 8, own.at[1], 0, 4)
        put(cot, 12, oth.at[1], 0, 4)
        put(cot, 16, near_other.at[1], 4, 4)

    @pl.when(core == 1)
    def _():
        put(crop, 0, far_other, 4, 4)
        put(crop, 4, near_other.at[0], 0, 8)
        put(crop, 12, oth.at[0], 0, 4)
        put(crop, 16, own.at[0], 0, 4)
        put(crop, 20, near.at[0], 4, 4)
        put(crop, 24, near.at[0], 0, 4)
        put(crop, 28, far, 4, 4)
        put(crop, 32, far, 0, 4)
        put(cot, 0, near_other.at[1], 4, 4)
        put(cot, 4, oth.at[1], 0, 4)
        put(cot, 8, own.at[1], 0, 4)
        put(cot, 12, near.at[1], 4, 4)
        put(cot, 16, near.at[1], 0, 4)

    def conv(src, matrix, low, high, then):
        rows = range(low, high, 2)
        for at in range(0, len(rows), PAIRS):
            some = rows[at : at + PAIRS]
            product[at * WIDTH : (at + len(some)) * WIDTH, :] = jnp.dot(
                stacked(src, [row - 1 for row in some], 4), matrix[...], preferred_element_type=F32
            )

            def finish(i, row):
                for r in range(2):
                    block = product.at[i * WIDTH : (i + 1) * WIDTH]
                    q = [block[:, (3 * r + b) * LANES : (3 * r + b + 1) * LANES] for b in range(3)]
                    here = slice((row + r) * WIDTH, (row + r + 1) * WIDTH)
                    then(here, q[1] + from_left(q[0]) + from_right(q[2]))

            for i, row in enumerate(some):
                finish(at + i, row)

    def clear_outside(dst, low, high, first=16):
        top = first - ROWS * gy
        bottom = first + ROWS * (lax.axis_size("gy") - gy)

        def clear(i, carry):
            dst[pl.ds(at_row(i), WIDTH), :] = jnp.zeros((WIDTH, LANES), BF16)
            return carry

        @pl.when(top > low)
        def _():
            lax.fori_loop(low, jnp.minimum(top, high), clear, 0)

        @pl.when(bottom < high)
        def _():
            lax.fori_loop(jnp.maximum(bottom, low), high, clear, 0)

    clear_outside(crop, 0, 36)
    clear_outside(cot, 0, 20, 8)

    for s in range(4):
        source = crop if s == 0 else feats.at[0] if s == 1 else merged.at[s - 2]

        def first(here, v, s=s):
            pre1[s, here, :] = v
            hidden[s, here, :] = (v * sigmoid(v)).astype(BF16)

        conv(source, w1.at[2 * s], 2 * s + 1, 35 - 2 * s, first)
        clear_outside(hidden.at[s], 2 * s + 1, 35 - 2 * s)

        def second(here, v, s=s):
            pre2[s, here, :] = v
            out = (v * sigmoid(v)).astype(BF16)
            feats[s, here, :] = out
            if s == 1 or s == 2:
                skip = feats[0, here, :] if s == 1 else crop[here, :]
                merged[s - 1, here, :] = (out.astype(F32) + skip.astype(F32)).astype(BF16)

        conv(hidden.at[s], w1.at[2 * s + 1], 2 * s + 2, 34 - 2 * s, second)
        if s == 0:
            clear_outside(feats.at[0], 2, 34)
        if s == 1 or s == 2:
            clear_outside(merged.at[s - 1], 2 * s + 2, 34 - 2 * s)

    here = slice(8 * WIDTH, 28 * WIDTH)
    sd[here, :] = (cot[...].astype(F32) * slope(pre2[3, here, :])).astype(BF16)

    own_low = half * 16
    base0 = 16 * WIDTH
    slot_of = lambda s: lax.rem(s - seg + 4, 4)

    def keep(index, src, grad):
        windows[index] = src[15 * WIDTH : 21 * WIDTH, :]
        deltas[index] = grad[16 * WIDTH : 20 * WIDTH, :]

    for s in (3, 2, 1, 0):
        source = crop if s == 0 else feats.at[0] if s == 1 else merged.at[s - 2]
        low, high = 8 + 2 * (3 - s), 28 - 2 * (3 - s)

        def to_first(here, v, s=s):
            fd[here, :] = (v * slope(pre1[s, here, :])).astype(BF16)

        keep(2 * s + 1, hidden.at[s], sd)
        conv(sd, wb.at[2 * s + 1], low + 1, high - 1, to_first)
        clear_outside(fd, low + 1, high - 1)
        keep(2 * s, source, fd)

        def to_delta(here, v, s=s):
            out = v.astype(BF16)
            if s == 1 or s == 0:
                other = delta[2 if s == 1 else 3, here, :]
                out = (out.astype(F32) + other.astype(F32)).astype(BF16)
            delta[s, here, :] = out
            if s > 0:
                sd[here, :] = (
                    out.astype(F32) * slope(pre2[s - 1, here, :])
                ).astype(BF16)

        conv(fd, wb.at[2 * s], low + 2, high - 2, to_delta)
        if s > 0:
            clear_outside(sd, low + 2, high - 2)

    for s in range(4):
        for y in range(ROWS):
            place = pl.ds(pl.multiple_of(base0 + y * WIDTH + own_low, 16), 64)
            out_all[slot_of(s), 64 * y : 64 * y + 64, :] = feats[s, place, :]
            out_all[slot_of(s), 256 + 64 * y : 320 + 64 * y, :] = delta[s, place, :]
    for k, out in enumerate((out0, out1, out2, out3)):
        out[...] = out_all[k]


def grads_kernel(windows, deltas, keep0, keep1, keep2, keep3, send, grads, terms, wg_all):
    seg = lax.axis_index("segment")
    core = lax.rem(lax.axis_index("gy"), 2)
    own_low = lax.div(seg, 2) * 16
    column = lax.broadcasted_iota(jnp.int32, (1, WIDTH, LANES), 1)
    mine = (column >= own_low) & (column < own_low + 64)
    _, collapse, on_plane = constants()
    for index in range(8):
        d = jnp.where(mine, by_rows(deltas[index].astype(F32)), 0.0).reshape(ROWS * WIDTH, LANES)
        shifted = jnp.concatenate([from_right(d).astype(BF16), d.astype(BF16), from_left(d).astype(BF16)], axis=1)
        product = lax.dot_general(
            stacked(windows.at[index], range(ROWS), 3), shifted, (((0,), (0,)), ((), ())), preferred_element_type=F32
        )
        for dx in range(3):
            grads[index, dx] = product[:, dx * LANES : (dx + 1) * LANES]
        top = 224 * index
        terms[top + 6 * 32 : top + 7 * 32, 3 * LANES :] = jnp.zeros((32, LANES), BF16)
        for dy in range(3):
            for dx in range(3):
                first = [dy * LANES + z * 32 for z in range(4)]
                rows = [grads[index, dx, at : at + 32, :] for at in first]
                for dz in range(3):
                    total = jnp.zeros((32, LANES), F32)
                    for z in range(4):
                        if 0 <= z + 1 - dz < 4:
                            total = jnp.where(on_plane[z + 1 - dz], rows[z], total)
                    t = 9 * dz + 3 * dy + dx
                    at = top + t // 4 * 32
                    terms[at : at + 32, t % 4 * LANES : (t % 4 + 1) * LANES] = total.astype(BF16)
    packed = jnp.dot(terms[...], collapse, preferred_element_type=F32).astype(BF16)
    for s in range(4):
        for which in range(2):
            top = 224 * (2 * s + which)
            wg_all[which, lax.rem(s - seg + 4, 4)] = packed[top : top + 224]
    for k, keep in enumerate((keep0, keep1, keep2, keep3)):
        keep[...] = wg_all[core, k]
    send[...] = wg_all[1 - core]


VMEM = pl.BlockSpec(memory_space=pltpu.VMEM)
MATRICES = (8, 4 * LANES, 6 * LANES)


def build_call(*packs):
    return pl.pallas_call(
        build_kernel,
        out_shape=[jax.ShapeDtypeStruct(MATRICES, BF16)] * 2,
        in_specs=[VMEM] * 7,
        out_specs=[VMEM] * 2,
        scratch_shapes=[
            pltpu.VMEM((4, 2, 224, LANES), BF16),
            pltpu.VMEM((224, 4 * LANES), F32),
            pltpu.VMEM((7 * LANES, LANES), F32),
        ],
        compiler_params=pltpu.CompilerParams(vmem_limit_bytes=8 * 1024 * 1024),
        cost_estimate=pl.CostEstimate(flops=5_000_000_000, bytes_accessed=10_000_000, transcendentals=0),
        name="banded",
    )(*packs)


def main_call(*operands):
    acts = (TOTAL * WIDTH, LANES)
    return pl.pallas_call(
        main_kernel,
        out_shape=[jax.ShapeDtypeStruct((512, LANES), BF16)] * 4
        + [
            jax.ShapeDtypeStruct((8, 6 * WIDTH, LANES), BF16),
            jax.ShapeDtypeStruct((8, 4 * WIDTH, LANES), BF16),
        ],
        in_specs=[VMEM] * 8,
        out_specs=[VMEM] * 6,
        scratch_shapes=[
            pltpu.VMEM(acts, BF16),
            pltpu.VMEM((20 * WIDTH, LANES), BF16),
            pltpu.VMEM((4,) + acts, BF16),
            pltpu.VMEM((2,) + acts, BF16),
            pltpu.VMEM((4,) + acts, BF16),
            pltpu.VMEM((4,) + acts, BF16),
            pltpu.VMEM(acts, BF16),
            pltpu.VMEM(acts, BF16),
            pltpu.VMEM((4,) + acts, F32),
            pltpu.VMEM((4,) + acts, F32),
            pltpu.VMEM((17 * WIDTH, 6 * LANES), F32),
            pltpu.VMEM((4, 512, LANES), BF16),
        ],
        compiler_params=pltpu.CompilerParams(vmem_limit_bytes=36 * 1024 * 1024),
        cost_estimate=pl.CostEstimate(flops=20_000_000_000, bytes_accessed=10_000_000, transcendentals=0),
        name="sections",
    )(*operands)


def grads_call(windows, deltas):
    return pl.pallas_call(
        grads_kernel,
        out_shape=[jax.ShapeDtypeStruct((224, LANES), BF16)] * 4 + [jax.ShapeDtypeStruct((4, 224, LANES), BF16)],
        in_specs=[VMEM] * 2,
        out_specs=[VMEM] * 5,
        scratch_shapes=[
            pltpu.VMEM((8, 3, 3 * LANES, LANES), F32),
            pltpu.VMEM((8 * 224, 4 * LANES), BF16),
            pltpu.VMEM((2, 4, 224, LANES), BF16),
        ],
        compiler_params=pltpu.CompilerParams(vmem_limit_bytes=16 * 1024 * 1024),
        cost_estimate=pl.CostEstimate(flops=6_000_000_000, bytes_accessed=4_000_000, transcendentals=0),
        name="kernel_grads",
    )(windows, deltas)


def layout_kernel(in0, in1, in2, in3, features, gradients, by_source):
    seg = lax.axis_index("segment")
    for k, arrived in enumerate((in0, in1, in2, in3)):
        by_source[lax.rem(seg - k + 4, 4)] = arrived[...]
    for which, out in enumerate((features, gradients)):
        for m in range(2):
            planes = []
            for y in range(ROWS):
                start = 256 * which + 64 * y
                row = jnp.concatenate([by_source[m, start : start + 64, :], by_source[2 + m, start : start + 64, :]])
                planes.append(row.astype(F32).T[:, None, :])
            for z in range(4):
                part = [plane[32 * z : 32 * z + 32] for plane in planes]
                out[m, :, z] = jnp.concatenate(part, axis=1).astype(out.dtype)


def layout_call(*arrived):
    return pl.pallas_call(
        layout_kernel,
        out_shape=[
            jax.ShapeDtypeStruct((2, 32, 4, ROWS, LANES), BF16),
            jax.ShapeDtypeStruct((2, 32, 4, ROWS, LANES), F32),
        ],
        in_specs=[VMEM] * 4,
        out_specs=[VMEM] * 2,
        scratch_shapes=[pltpu.VMEM((4, 512, LANES), BF16)],
        compiler_params=pltpu.CompilerParams(vmem_limit_bytes=8 * 1024 * 1024),
        cost_estimate=pl.CostEstimate(flops=4_000_000_000, bytes_accessed=4_000_000, transcendentals=0),
        name="layout",
    )(*arrived)


def rotated(value, axis, group, step, stride):
    count = lax.axis_size(axis)

    def target(i):
        place = i // stride % group
        return i + ((place + step) % group - place) * stride

    return lax.ppermute(value, axis, [(i, target(i)) for i in range(count)])


def local(crops, cotangent, weights):
    micro_count, channels, planes, rows, across = crops.shape
    seg = lax.axis_index("segment")
    micro, half = seg % 2, seg // 2
    devices = lax.axis_size("gy")
    swap = [(i, i ^ 1) for i in range(devices)]

    def tile(volume):
        field = lax.dynamic_index_in_dim(volume, micro, 0, keepdims=False)
        field = jnp.transpose(field, (2, 3, 1, 0)).reshape(rows, across, channels * planes)
        return lax.dynamic_slice_in_dim(field, half * 48, WIDTH, 1).reshape(rows * WIDTH, channels * planes)

    own = jnp.stack([tile(crops), tile(cotangent)])
    packed = jnp.pad(weights[0], ((0, 0), (0, 1), (0, 0), (0, 0))).reshape(2, 7, 4, channels, channels)
    packed = jnp.transpose(packed, (0, 1, 3, 2, 4)).reshape(2, 7 * channels, 4 * channels)

    share = lax.dynamic_index_in_dim(packed, lax.axis_index("gy") % 2, 0, keepdims=False)
    one, three, two = [rotated(share, "segment", 4, k, 1) for k in (1, 3, 2)]
    others = [one, two, three]
    others += [lax.ppermute(other, "gy", swap) for other in others]
    oth = lax.ppermute(own, "gy", swap)
    oth, packed = lax.optimization_barrier((oth, packed))
    block = jnp.concatenate([own, oth], axis=1)

    def outward(distance):
        return [(i, (i + 2 * distance * (1 if i % 2 == 0 else -1)) % devices) for i in range(devices)]

    near = lax.ppermute(block, "gy", outward(1))
    far = lax.ppermute(block[0], "gy", outward(2))
    w1, wb = build_call(packed, *others)
    near_other = lax.ppermute(near, "gy", swap)
    far_other = lax.ppermute(far, "gy", swap)
    outs = main_call(own, oth, near, far, near_other, far_other, w1, wb)
    fields = outs[:4]
    arrived = [rotated(fields[k], "segment", 4, k, 1) for k in (1, 2, 3)]
    *keep, send = grads_call(outs[4], outs[5])

    got = lax.ppermute(send, "gy", swap)
    part = [(keep[k].astype(F32) + got[k].astype(F32)).astype(BF16) for k in range(4)]
    total = part[0].astype(F32)
    for k in (2, 1, 3):
        total = total + rotated(part[k], "segment", 4, k, 1).astype(F32)
    for stride in (2, 8):
        mine = total.astype(BF16)
        total = mine.astype(F32)
        for k in (1, 2, 3):
            total = total + rotated(mine, "gy", 4, k, stride).astype(F32)
    features, input_grads = layout_call(fields[0], *arrived)
    mine, features, input_grads = lax.optimization_barrier((total.astype(BF16), features, input_grads))
    other = lax.ppermute(mine, "gy", swap)
    low_core = lax.axis_index("gy") % 2 == 0
    both = jnp.stack([jnp.where(low_core, mine, other), jnp.where(low_core, other, mine)])
    grads = both.reshape(2, 7, channels, 4, channels).transpose(0, 1, 3, 2, 4)
    grads = grads.reshape(2, 28, channels, channels)[:, :27].astype(F32)

    shape = (1, micro_count, channels, planes, rows, across)
    return features.reshape(shape), grads[None], input_grads.reshape(shape)


def solution(mesh):
    return jax.shard_map(
        local,
        mesh=mesh,
        in_specs=(
            P(None, None, None, "gy", None),
            P(None, None, None, "gy", None),
            P("segment", None, None, None, None),
        ),
        out_specs=(
            P("segment", None, None, None, "gy", None),
            P("segment", None, None, None, None),
            P("segment", None, None, None, "gy", None),
        ),
        check_vma=False,
    )
```
